256 devices in a mesh: tm: 64 (over z, y_hi, x), row: 2 (over core), col: 2 (over y_lo).
Axes of the slice: x: 4, y: 4 (y_hi: 2, y_lo: 2; y = y_hi * 2 + y_lo), z: 8, core: 2. Of those that a mesh axis runs over, the one named last changes fastest.
Arguments:
- frames_in: bfloat16 [1024, 16, 32, 256], P('tm', 'row', 'col'), may hold values from -6 to 6
- norm_gain: float32 [256], replicated, may hold values from 0.1 to 1.9
- conv_space: bfloat16 [3, 3, 256, 256], replicated, may hold values from -0.125 to 0.125
- conv_time: bfloat16 [3, 256, 256], replicated, may hold values from -0.21875 to 0.21875
- attn_gain: float32 [256], replicated, may hold values from 0.1 to 1.9
- query_weight: bfloat16 [256, 256], replicated, may hold values from -2 to 2
- key_weight: bfloat16 [256, 256], replicated, may hold values from -2 to 2
- value_weight: bfloat16 [256, 256], replicated, may hold values from -0.375 to 0.375
- out_weight: bfloat16 [256, 256], replicated, may hold values from -0.375 to 0.375
Outputs:
- block_out: bfloat16 [1024, 16, 32, 256], P('tm', 'row', 'col')
The draws below stay inside these ranges and needn't reach their ends.
All inputs are finite; a program needn't handle non-finite values.
Results may differ from the reference program's by a relative error of at most 0.0085.
Values may be sent and summed in bfloat16 or wider, within the bound.
A program may use at most 128 MiB of HBM per device.

```python
import jax
import jax.numpy as jnp
from jax import lax

C = 256
HEADS = 8
WINDOW = 32
FB = 16
FRAMES = 1024
HEIGHT = 16
WIDTH = 32


def draw_query_weight(key, part):
    key = jax.random.fold_in(key, 1)
    own = jnp.clip(jax.random.normal(key, (C, C), jnp.float32), -4.0, 4.0) / jnp.sqrt(jnp.float32(C))
    result = own
    return jnp.clip(result, -2.0, 2.0).astype(jnp.bfloat16)


def draw_key_weight(key, part):
    key = jax.random.fold_in(key, 2)
    own = jnp.clip(jax.random.normal(key, (C, C), jnp.float32), -4.0, 4.0) / jnp.sqrt(jnp.float32(C))
    result = own
    return jnp.clip(result, -2.0, 2.0).astype(jnp.bfloat16)


def block_scale(key, shape, cuts, least, top_value):
    def one(dim, shards_of):
        draws = jax.random.uniform(jax.random.fold_in(jax.random.fold_in(key, 6), dim), (shards_of,), jnp.float32, least / len(cuts), top_value / len(cuts))
        return jnp.repeat(jnp.exp(draws), shape[dim] // shards_of).reshape((-1,) + (1,) * (len(shape) - dim - 1))

    factor_of = one(*cuts[0])
    for cut in cuts[1:]:
        factor_of = factor_of * one(*cut)
    return factor_of


def gaussian(stream_key, extent, scale, reach, split=(), kind=jnp.bfloat16):
    entries = jax.random.normal(stream_key, extent, jnp.float32) * scale
    if len(split) > 0:
        entries = block_scale(stream_key, extent, split, -0.22, 0.18) * entries
    return jnp.clip(entries, min=-reach, max=reach).astype(kind)


def setup_inputs(seed: int = 0) -> dict:
    streams_of = jax.random.split(jax.random.key(seed), 10)
    return {
        "frames_in": gaussian(streams_of[0], (FRAMES, HEIGHT, WIDTH, C), 1.0, 6.0, ((0, 64), (1, 2), (2, 2))),
        "norm_gain": jnp.clip(1.0 + 0.18 * jax.random.normal(streams_of[1], (C,), jnp.float32), 0.1, 1.9),
        "conv_space": gaussian(streams_of[2], (3, 3, C, C), (9 * C) ** -0.5, 0.125),
        "conv_time": gaussian(streams_of[3], (3, C, C), (3 * C) ** -0.5, 0.21875),
        "attn_gain": jnp.clip(1.0 + 0.18 * jax.random.normal(streams_of[4], (C,), jnp.float32), 0.1, 1.9),
        "query_weight": draw_query_weight(jax.random.fold_in(streams_of[9], 71), 0),
        "key_weight": draw_key_weight(jax.random.fold_in(streams_of[9], 71), 0),
        "value_weight": gaussian(streams_of[7], (C, C), C ** -0.5, 0.375),
        "out_weight": gaussian(streams_of[8], (C, C), C ** -0.5, 0.375),
    }


def rms_norm(values, gain):
    wide = values.astype(jnp.float32)
    scaled = wide * lax.rsqrt(lax.optimization_barrier(jnp.mean(wide * wide, axis=-1, keepdims=True)) + 1e-06)
    return (scaled * gain.astype(jnp.float32)).astype(jnp.bfloat16)

def spatial_conv(normed, conv_space):
    height = normed.shape[1]
    width = normed.shape[2]
    padded = jnp.pad(normed, ((0, 0), (1, 1), (1, 1), (0, 0)))
    total = jnp.zeros(normed.shape, jnp.float32)
    for shift_y in range(3):
        for shift_x in range(3):
            window = padded[:, shift_y:shift_y + height, shift_x:shift_x + width, :]
            total = total + jnp.dot(window, conv_space[shift_y, shift_x], preferred_element_type=jnp.float32)
    return jax.nn.silu(total).astype(jnp.bfloat16)

def reference(frames_in, norm_gain, conv_space, conv_time, attn_gain, query_weight, key_weight, value_weight, out_weight):
    frames, height, width, chans = frames_in.shape
    blocks = frames // FB
    positions = height * width
    head_size = chans // HEADS
    normed = rms_norm(frames_in, norm_gain)
    spatial = lax.map(lambda piece: spatial_conv(piece, conv_space), normed.reshape(blocks, FB, height, width, chans))
    spatial = spatial.reshape(frames, height, width, chans)
    padded = jnp.concatenate([jnp.zeros((2, height, width, chans), jnp.bfloat16), spatial], axis=0)
    temporal = jnp.zeros(frames_in.shape, jnp.float32)
    for tap in range(3):
        temporal = temporal + jnp.dot(padded[2 - tap:2 - tap + frames], conv_time[tap], preferred_element_type=jnp.float32)
    hidden = (frames_in.astype(jnp.float32) + temporal).astype(jnp.bfloat16)
    attn_in = rms_norm(hidden, attn_gain)
    queries = jnp.dot(attn_in, query_weight, preferred_element_type=jnp.float32).astype(jnp.bfloat16)
    keys = jnp.dot(attn_in, key_weight, preferred_element_type=jnp.float32).astype(jnp.bfloat16)
    values = jnp.dot(attn_in, value_weight, preferred_element_type=jnp.float32).astype(jnp.bfloat16)
    queries = queries.reshape(frames, positions, HEADS, head_size)
    front = jnp.zeros((WINDOW, positions, HEADS, head_size), jnp.bfloat16)
    keys = jnp.concatenate([front, keys.reshape(frames, positions, HEADS, head_size)], axis=0)
    values = jnp.concatenate([front, values.reshape(frames, positions, HEADS, head_size)], axis=0)
    scale = head_size ** (-0.5)
    span = FB + WINDOW

    def attend(block):
        start = (block * FB).astype(jnp.int32)
        query_block = lax.dynamic_slice_in_dim(queries, start, FB, 0).astype(jnp.float32)
        key_block = lax.dynamic_slice_in_dim(keys, start, span, 0).astype(jnp.float32)
        value_block = lax.dynamic_slice_in_dim(values, start, span, 0).astype(jnp.float32)
        scores = jnp.einsum('iphd,jphd->phij', query_block, key_block) * scale
        query_frame = start + jnp.arange(FB, dtype=jnp.int32)[:, None]
        key_frame = start - WINDOW + jnp.arange(span, dtype=jnp.int32)[None, :]
        valid = (key_frame <= query_frame) & (key_frame > query_frame - WINDOW) & (key_frame >= 0)
        scores = jnp.where(valid, scores, -1e+30)
        top = lax.optimization_barrier(jnp.max(scores, axis=-1, keepdims=True))
        expo = jnp.exp(scores - top)
        weights = (expo / lax.optimization_barrier(jnp.sum(expo, axis=-1, keepdims=True))).astype(jnp.bfloat16)
        mixed = jnp.einsum('phij,jphd->iphd', weights.astype(jnp.float32), value_block)
        return mixed.astype(jnp.bfloat16)
    mixed = lax.map(attend, jnp.arange(blocks, dtype=jnp.int32)).reshape(frames, height, width, chans)
    result = hidden.astype(jnp.float32) + jnp.dot(mixed, out_weight, preferred_element_type=jnp.float32)
    return result.astype(jnp.bfloat16)
```

```python
import functools

import jax
import jax.numpy as jnp
from jax import lax
from jax.experimental import pallas as pl
from jax.experimental.pallas import tpu as pltpu
from jax.sharding import PartitionSpec as P

HEADS = 8
WINDOW = 32
RING = 4
BANDS = 4
MESH = pl.DeviceIdType.MESH
F32 = jnp.float32
BF16 = jnp.bfloat16


def dot(a, b):
    return jnp.dot(a, b, preferred_element_type=F32)


def iota(shape, dim):
    return lax.broadcasted_iota(jnp.int32, shape, dim)


def kernel(
    tm_count,
    x_hbm, ng_ref, cs_hbm, ct_hbm, ag_ref, wq_hbm, wk_hbm, wv_hbm, wo_hbm,
    out_hbm,
    xs, cs, ct, wqkv, wo,
    perm, pick, place, bias, hmask,
    ext, xp, sp, hsend, hrecv, hidden, abuf, xall, qb, kb, vb, mb, mback, res, ov,
    load_sem, store_sem, rim_send, rim_recv, th_send, th_recv,
    a1_send, a1_recv, fw_send, fw_recv, a2_send, a2_recv,
):
    tm, row, col = (lax.axis_index(a) for a in ("tm", "row", "col"))
    ring, group = lax.rem(tm, RING), lax.div(tm, RING)
    groups = tm_count // RING

    def ring_at(k):
        return {"tm": group * RING + lax.rem(ring + k, RING)}

    core = {"row": 1 - row}
    side = {"col": 1 - col}
    diag = {"row": 1 - row, "col": 1 - col}
    tm_next = {"tm": lax.rem(tm + 1, tm_count)}
    tm_prev = {"tm": lax.rem(tm + tm_count - 1, tm_count)}
    group_next = {"tm": lax.rem(group + 1, groups) * RING + ring}
    group_prev = {"tm": lax.rem(group + groups - 1, groups) * RING + ring}

    loads = [
        pltpu.make_async_copy(src, dst, load_sem.at[i])
        for i, (src, dst) in enumerate(
            [
                (x_hbm, xs), (cs_hbm, cs), (ct_hbm, ct), (wq_hbm, wqkv.at[0]),
                (wk_hbm, wqkv.at[1]), (wv_hbm, wqkv.at[2]), (wo_hbm, wo),
            ]
        )
    ]
    for load in loads:
        load.start()

    barrier = pltpu.get_barrier_semaphore()
    partners = (
        core, side, diag, ring_at(1), ring_at(2), ring_at(3),
        tm_next, tm_prev, group_next, group_prev,
    )
    for partner in partners:
        pl.semaphore_signal(barrier, inc=1, device_id=partner, device_id_type=MESH)

    def remote(src, dst, send, recv, where):
        return pltpu.make_async_remote_copy(
            src_ref=src, dst_ref=dst, send_sem=send, recv_sem=recv,
            device_id=where, device_id_type=MESH,
        )

    r, s = iota((256, 256), 0), iota((256, 256), 1)
    perm[...] = (((r >> 4) == (s & 15)) & ((r & 15) == (s >> 4))).astype(F32).astype(BF16)
    r, s = iota((32, 256), 0), iota((32, 256), 1)
    pick[...] = (s == (r & 15) * 16 + 14 + (r >> 4)).astype(F32).astype(BF16)
    r, s = iota((512, 32), 0), iota((512, 32), 1)
    lag, cell, frame = r >> 8, (r >> 4) & 15, r & 15
    hit = (s == (frame + 1 - lag) * 16 + cell) & (frame <= lag) & (tm > 0)
    place[...] = hit.astype(F32).astype(BF16)
    key, query = iota((48, 128), 0), iota((48, 128), 1) & 15
    for b in range(3):
        first = jnp.where(group == 0, max(0, 32 - 16 * b), 0)
        seen = (key > query) & (key <= query + 32) & (key >= first)
        bias[b] = jnp.where(seen, 0.0, -1e30).astype(F32)
    h, lane = iota((HEADS, 16, 256), 0), iota((HEADS, 16, 256), 2)
    hmask[...] = (h == (lane >> 5)).astype(F32).astype(BF16)
    ext[9 * row] = jnp.zeros((18, 16, 256), BF16)
    for y in range(10):
        ext[y, 17 * col] = jnp.zeros((16, 256), BF16)

    loads[0].wait()
    pl.semaphore_wait(barrier, len(partners))

    def norm_row(i):
        y = (i + 7 * (1 - row)) & 7
        v = dot(perm[...], xs[:, y].reshape(256, 256))
        scale = lax.rsqrt(jnp.mean(v * v, axis=-1, keepdims=True) + 1e-6)
        ext[y + 1, pl.ds(1, 16)] = (v * scale * ng_ref[...]).astype(BF16).reshape(16, 16, 256)
        xp[y] = v.astype(BF16).reshape(16, 16, 256)

    norm_row(0)
    rim_y, rim_x = 8 - 7 * row, 16 - 15 * col
    rims = [
        remote(
            ext.at[rim_y, pl.ds(1, 16)], ext.at[9 * row, pl.ds(1, 16)],
            rim_send.at[0], rim_recv.at[0], core,
        ),
        remote(
            ext.at[rim_y, rim_x], ext.at[9 * row, 17 * col],
            rim_send.at[1], rim_recv.at[1], diag,
        ),
        remote(
            ext.at[pl.ds(1, 8), rim_x], ext.at[pl.ds(1, 8), 17 * col],
            rim_send.at[2], rim_recv.at[2], side,
        ),
    ]
    rims[0].start()
    rims[1].start()

    @pl.loop(1, 8)
    def _(i):
        norm_row(i)

    rims[2].start()
    loads[1].wait()
    loads[2].wait()

    def band_column(band):
        return 4 * band + col * (12 - 8 * band)

    def conv(band, half):
        y0, c0 = 4 * ((half + row) & 1), band_column(band)
        total = None
        for dy in range(3):
            for dx in range(3):
                cells = ext[pl.ds(y0 + dy, 4), pl.ds(c0 + dx, 4)].reshape(256, 256)
                term = dot(cells, cs[dy, dx])
                total = term if total is None else total + term
        act = (0.5 * total * (1.0 + jnp.tanh(0.5 * total))).astype(BF16)
        sp[band, half] = act
        hsend[band, half] = dot(pick[...], act).astype(BF16)

    def tm_copy(band):
        return remote(
            hsend.at[band], hrecv.at[band], th_send.at[band], th_recv.at[band], tm_next
        )

    def temporal(band, half):
        q0, c0 = 2 * ((half + row) & 1), band_column(band)
        act = sp[band, half]
        wide = act.astype(F32).reshape(16, 16, 256)
        early = dot(place[...], hrecv[band, half])
        frame = iota((16, 16, 256), 1)
        total = dot(act, ct[0])
        for lag in (1, 2):
            before = early[256 * (lag - 1) : 256 * lag].reshape(16, 16, 256)
            moved = jnp.where(frame < lag, before, pltpu.roll(wide, lag, 1))
            total = total + dot(moved.astype(BF16).reshape(256, 256), ct[lag])
        own = xp[pl.ds(2 * q0, 4), pl.ds(c0, 4)].reshape(256, 256).astype(F32)
        hid = (own + total).astype(BF16)
        hidden[band, pl.ds(q0, 2)] = hid.reshape(2, 128, 256)
        v = hid.astype(F32)
        scale = lax.rsqrt(jnp.mean(v * v, axis=-1, keepdims=True) + 1e-6)
        abuf[band, pl.ds(q0, 2)] = (v * scale * ag_ref[...]).astype(BF16).reshape(2, 128, 256)

    def a1_copy(band, k):
        to = lax.rem(ring + k, RING)
        return remote(
            abuf.at[band, to], xall.at[band, 2 + ring],
            a1_send.at[band, k - 1], a1_recv.at[band, k - 1], ring_at(k),
        )

    @pl.loop(0, BANDS + 2)
    def _(i):
        @pl.when(i == 0)
        def _():
            rims[0].wait()
            rims[1].wait()

        @pl.when(i == BANDS - 1)
        def _():
            rims[2].wait()

        @pl.when(i < BANDS)
        def _():
            @pl.loop(0, 2)
            def _(half):
                conv(i, half)

            tm_copy(i).start()

        @pl.when(i >= 2)
        def _():
            band = i - 2
            tm_copy(band).wait()

            @pl.loop(0, 2)
            def _(half):
                temporal(band, half)

            for k in (1, 2, 3):
                a1_copy(band, k).start()
            xall[band, 2 + ring] = abuf[band, ring]

    def forward(band):
        return remote(
            xall.at[band, pl.ds(4, 2)], xall.at[band, pl.ds(0, 2)],
            fw_send.at[band], fw_recv.at[band], group_next,
        )

    def a2_copy(band, k):
        to = lax.rem(ring + k, RING)
        return remote(
            mb.at[band, to], mback.at[band, ring],
            a2_send.at[band, k - 1], a2_recv.at[band, k - 1], ring_at(k),
        )

    for i in (3, 4, 5, 6):
        loads[i].wait()

    def keys_values(band, block):
        tokens = xall[band, block]
        kb[band, block] = dot(tokens, wqkv[1]).astype(BF16).reshape(8, 16, 256)
        vb[band, block] = dot(tokens, wqkv[2]).astype(BF16).reshape(8, 16, 256)

    def attend(band, cell, block):
        query = qb[band, block, cell]
        spread = (query[None] * hmask[...]).reshape(128, 256)
        keys = kb[band, pl.ds(block, 3), cell].reshape(48, 256)
        values = vb[band, pl.ds(block, 3), cell].reshape(48, 256)
        scores = lax.dot_general(
            keys, spread, (((1,), (1,)), ((), ())), preferred_element_type=F32
        )
        scores = scores * (1.4426950408889634 * 32**-0.5) + bias[min(block, 2)]
        expo = jnp.exp2(scores - jnp.max(scores, axis=0, keepdims=True))
        weights = expo * (1.0 / jnp.sum(expo, axis=0, keepdims=True))
        mixed = lax.dot_general(
            weights.astype(BF16), values, (((0,), (0,)), ((), ())), preferred_element_type=F32
        )
        mixed = mixed.reshape(HEADS, 16, 256)
        parts = []
        for lanes in (slice(0, 128), slice(128, 256)):
            first = lanes.start // 32
            lane = iota((16, 128), 1) >> 5
            part = mixed[first, :, lanes]
            for h in range(1, 4):
                part = jnp.where(lane == h, mixed[first + h, :, lanes], part)
            parts.append(part)
        mb[band, block, pl.ds(pl.multiple_of(cell * 16, 16), 16)] = jnp.concatenate(
            parts, axis=-1
        ).astype(BF16)

    @pl.loop(0, BANDS + 1)
    def _(i):
        @pl.when(i < BANDS)
        def _():
            for k in (1, 2, 3):
                a1_copy(i, k).wait()
            forward(i).start()

            @pl.loop(0, 4)
            def _(block):
                qb[i, block] = (
                    dot(xall[i, block + 2], wqkv[0]).astype(BF16).reshape(8, 16, 256)
                )
                keys_values(i, block + 2)

        @pl.when(i >= 1)
        def _():
            band = i - 1
            forward(band).wait()

            @pl.loop(0, 2)
            def _(block):
                keys_values(band, block)

            @pl.loop(0, 8)
            def _(cell):
                for block in range(4):
                    attend(band, cell, block)

            for k in (1, 2, 3):
                a2_copy(band, k).start()
            mback[band, ring] = mb[band, ring]

    @pl.loop(0, BANDS)
    def _(band):
        for k in (1, 2, 3):
            a2_copy(band, k).wait()
        c0 = band_column(band)

        @pl.loop(0, 4)
        def _(q):
            total = hidden[band, q].astype(F32) + dot(mback[band, q], wo[...])
            res[pl.ds(2 * q, 2), pl.ds(c0, 4)] = total.astype(BF16).reshape(2, 4, 16, 256)

    @pl.loop(0, 8)
    def _(y):
        o = dot(perm[...], res[y].reshape(256, 256)).astype(BF16)
        ov[:, y] = o.reshape(16, 16, 256)

    store = pltpu.make_async_copy(ov, out_hbm, store_sem.at[0])
    store.start()
    store.wait()


def solution(mesh):
    tm_count = mesh.shape["tm"]

    def step(x, norm_gain, conv_space, conv_time, attn_gain, wq, wk, wv, wo):
        def vmem(*shape, dtype=BF16):
            return pltpu.VMEM(shape, dtype)

        dma = pltpu.SemaphoreType.DMA
        anywhere = pl.BlockSpec(memory_space=pl.ANY)
        here = pl.BlockSpec(memory_space=pltpu.VMEM)
        return pl.pallas_call(
            functools.partial(kernel, tm_count),
            out_shape=jax.ShapeDtypeStruct(x.shape, x.dtype),
            in_specs=[
                anywhere, here, anywhere, anywhere, here,
                anywhere, anywhere, anywhere, anywhere,
            ],
            out_specs=anywhere,
            scratch_shapes=[
                vmem(16, 8, 16, 256), vmem(3, 3, 256, 256), vmem(3, 256, 256),
                vmem(3, 256, 256), vmem(256, 256),
                vmem(256, 256), vmem(32, 256), vmem(512, 32), vmem(3, 48, 128, dtype=F32),
                vmem(HEADS, 16, 256),
                vmem(10, 18, 16, 256), vmem(8, 16, 16, 256), vmem(BANDS, 2, 256, 256),
                vmem(BANDS, 2, 32, 256), vmem(BANDS, 2, 32, 256), vmem(BANDS, 4, 128, 256),
                vmem(BANDS, 4, 128, 256), vmem(BANDS, 6, 128, 256),
                vmem(BANDS, 4, 8, 16, 256), vmem(BANDS, 6, 8, 16, 256),
                vmem(BANDS, 6, 8, 16, 256), vmem(BANDS, 4, 128, 256),
                vmem(BANDS, 4, 128, 256), vmem(8, 16, 16, 256), vmem(16, 8, 16, 256),
                dma((7,)), dma((1,)), dma((3,)), dma((3,)), dma((BANDS,)), dma((BANDS,)),
                dma((BANDS, 3)), dma((BANDS, 3)), dma((BANDS,)), dma((BANDS,)),
                dma((BANDS, 3)), dma((BANDS, 3)),
            ],
            compiler_params=pltpu.CompilerParams(
                collective_id=0, has_side_effects=True, vmem_limit_bytes=48 << 20
            ),
            name="encoder_block",
        )(
            x, norm_gain.reshape(1, -1), conv_space, conv_time, attn_gain.reshape(1, -1),
            wq, wk, wv, wo,
        )

    tile = P("tm", "row", "col", None)
    return jax.shard_map(
        step,
        mesh=mesh,
        in_specs=(tile, P(), P(), P(), P(), P(), P(), P(), P()),
        out_specs=tile,
        check_vma=False,
    )
```

```python
import functools

import jax
import jax.numpy as jnp
from jax import lax
from jax.experimental import pallas as pl
from jax.experimental.pallas import tpu as pltpu
from jax.sharding import PartitionSpec as P

RING = 4
BANDS = 4
MESH = pl.DeviceIdType.MESH
F32 = jnp.float32
BF16 = jnp.bfloat16


def dot(a, b):
    return jnp.dot(a, b, preferred_element_type=F32)


def iota(shape, dim):
    return lax.broadcasted_iota(jnp.int32, shape, dim)


def kernel(
    tm_count,
    x_hbm, ng_ref, cs_hbm, ct_hbm, ag_ref, wq_hbm, wk_hbm, wv_hbm, wo_hbm,
    out_hbm,
    xs, cs, ct, wqkv, wo,
    perm, pick, place, bias, hmask,
    ext, xp, sp, hsend, hrecv, hidden, abuf, xall, qb, kb, vb, mb, mback, res, ov,
    load_sem, store_sem, rim_send, rim_recv, th_send, th_recv,
    a1_send, a1_recv, fw_send, fw_recv, a2_send, a2_recv,
):
    tm, row, col = (lax.axis_index(a) for a in ("tm", "row", "col"))
    ring, group = lax.rem(tm, RING), lax.div(tm, RING)
    groups = tm_count // RING

    def ring_at(k):
        return {"tm": group * RING + lax.rem(ring + k, RING)}

    core = {"row": 1 - row}
    side = {"col": 1 - col}
    diag = {"row": 1 - row, "col": 1 - col}
    tm_next = {"tm": lax.rem(tm + 1, tm_count)}
    tm_prev = {"tm": lax.rem(tm + tm_count - 1, tm_count)}
    group_next = {"tm": lax.rem(group + 1, groups) * RING + ring}
    group_prev = {"tm": lax.rem(group + groups - 1, groups) * RING + ring}

    row_halves = (4 * (1 - row), 4 * row)
    loads = [
        pltpu.make_async_copy(src, dst, load_sem.at[i])
        for i, (src, dst) in enumerate(
            [(x_hbm.at[:, pl.ds(y0, 4)], xs.at[:, pl.ds(y0, 4)]) for y0 in row_halves]
            + [
                (cs_hbm, cs), (ct_hbm, ct), (wq_hbm, wqkv.at[0]),
                (wk_hbm, wqkv.at[1]), (wv_hbm, wqkv.at[2]), (wo_hbm, wo),
            ]
        )
    ]
    for load in loads:
        load.start()

    barrier = pltpu.get_barrier_semaphore()
    partners = (
        core, side, diag, ring_at(1), ring_at(2), ring_at(3),
        tm_next, tm_prev, group_next, group_prev,
    )
    for partner in partners:
        pl.semaphore_signal(barrier, inc=1, device_id=partner, device_id_type=MESH)

    def remote(src, dst, send, recv, where):
        return pltpu.make_async_remote_copy(
            src_ref=src, dst_ref=dst, send_sem=send, recv_sem=recv,
            device_id=where, device_id_type=MESH,
        )

    r, s = iota((256, 256), 0), iota((256, 256), 1)
    perm[...] = (((r >> 4) == (s & 15)) & ((r & 15) == (s >> 4))).astype(F32).astype(BF16)
    r, s = iota((32, 256), 0), iota((32, 256), 1)
    pick[...] = (s == (r & 15) * 16 + 14 + (r >> 4)).astype(F32).astype(BF16)
    r, s = iota((512, 32), 0), iota((512, 32), 1)
    lag, cell, frame = r >> 8, (r >> 4) & 15, r & 15
    hit = (s == (frame + 1 - lag) * 16 + cell) & (frame <= lag) & (tm > 0)
    place[...] = hit.astype(F32).astype(BF16)
    key, lane = iota((128, 128), 0) & 63, iota((128, 128), 1)
    query = (lane & 15) + 16 * (lane >> 6)
    for half in range(2):
        first = jnp.where(group == 0, 32 - 32 * half, 0)
        seen = (key > query) & (key <= query + 32) & (key >= first)
        bias[half] = jnp.where(seen, 0.0, -1e30).astype(F32)
    h, lane = iota((4, 16, 256), 0), iota((4, 16, 256), 2)
    hmask[...] = (h == ((lane >> 5) & 3)).astype(F32).astype(BF16)
    ext[9 * row] = jnp.zeros((18, 16, 256), BF16)
    for y in range(10):
        ext[y, 17 * col] = jnp.zeros((16, 256), BF16)

    @jax.named_scope("norm_rows")
    def norm_rows(half):
        loads[half].wait()
        for i in range(4):
            y = row_halves[half] + i
            v = dot(perm[...], xs[:, y].reshape(256, 256))
            scale = lax.rsqrt(jnp.mean(v * v, axis=-1, keepdims=True) + 1e-6)
            ext[y + 1, pl.ds(1, 16)] = (v * scale * ng_ref[...]).astype(BF16).reshape(16, 16, 256)
            xp[y] = v.astype(BF16).reshape(16, 16, 256)

    norm_rows(0)
    with jax.named_scope("barrier"):
        pl.semaphore_wait(barrier, len(partners))
    rim_y, rim_x = 8 - 7 * row, 16 - 15 * col
    rims = [
        remote(
            ext.at[rim_y, pl.ds(1, 16)], ext.at[9 * row, pl.ds(1, 16)],
            rim_send.at[0], rim_recv.at[0], core,
        ),
        remote(
            ext.at[rim_y, rim_x], ext.at[9 * row, 17 * col],
            rim_send.at[1], rim_recv.at[1], diag,
        ),
        remote(
            ext.at[pl.ds(1, 8), rim_x], ext.at[pl.ds(1, 8), 17 * col],
            rim_send.at[2], rim_recv.at[2], side,
        ),
    ]
    rims[0].start()
    rims[1].start()

    norm_rows(1)
    rims[2].start()
    loads[2].wait()
    loads[3].wait()

    def band_column(band):
        return 4 * band + col * (12 - 8 * band)

    @jax.named_scope("conv")
    def conv(band):
        c0 = band_column(band)
        total = None
        for dy in range(3):
            for dx in range(3):
                cells = ext[dy : dy + 8, pl.ds(c0 + dx, 4)].reshape(512, 256)
                term = dot(cells, cs[dy, dx])
                total = term if total is None else total + term
        act = (0.5 * total * (1.0 + jnp.tanh(0.5 * total))).astype(BF16)
        sp[band] = act
        for half in range(2):
            last = dot(pick[...], act[256 * half : 256 * half + 256])
            hsend[band, half] = last.astype(BF16)

    def tm_copy(band):
        return remote(
            hsend.at[band], hrecv.at[band], th_send.at[band], th_recv.at[band], tm_next
        )

    @jax.named_scope("temporal")
    def temporal(band):
        act = sp[band]
        wide = act.astype(F32).reshape(32, 16, 256)
        early = [dot(place[...], hrecv[band, half]) for half in range(2)]
        frame = iota((32, 16, 256), 1)
        total = dot(act, ct[0])
        for lag in (1, 2):
            before = [e[256 * (lag - 1) : 256 * lag] for e in early]
            before = jnp.concatenate(before, axis=0).reshape(32, 16, 256)
            moved = jnp.where(frame < lag, before, pltpu.roll(wide, lag, 1))
            total = total + dot(moved.astype(BF16).reshape(512, 256), ct[lag])
        own = xp[:, pl.ds(band_column(band), 4)].reshape(512, 256).astype(F32)
        hid = (own + total).astype(BF16)
        hidden[band] = hid
        v = hid.astype(F32)
        scale = lax.rsqrt(jnp.mean(v * v, axis=-1, keepdims=True) + 1e-6)
        abuf[band] = (v * scale * ag_ref[...]).astype(BF16).reshape(4, 128, 256)

    def a1_copy(band, k):
        to = lax.rem(ring + k, RING)
        return remote(
            abuf.at[band, to], xall.at[band, 2 + ring],
            a1_send.at[band, k - 1], a1_recv.at[band, k - 1], ring_at(k),
        )

    @pl.loop(0, BANDS + 2)
    def _(i):
        @pl.when(i == 0)
        @jax.named_scope("rim_wait")
        def _():
            rims[0].wait()

        @pl.when(i == BANDS - 1)
        @jax.named_scope("rim_wait2")
        def _():
            rims[1].wait()
            rims[2].wait()

        @pl.when(i < BANDS)
        def _():
            conv(i)
            tm_copy(i).start()

        @pl.when(i >= 2)
        def _():
            band = i - 2
            with jax.named_scope("tm_wait"):
                tm_copy(band).wait()
            temporal(band)
            for k in (1, 2, 3):
                a1_copy(band, k).start()
            xall[band, 2 + ring] = abuf[band, ring]

    def forward(band):
        return remote(
            xall.at[band, pl.ds(4, 2)], xall.at[band, pl.ds(0, 2)],
            fw_send.at[band], fw_recv.at[band], group_next,
        )

    def a2_copy(band, k):
        to = lax.rem(ring + k, RING)
        return remote(
            mb.at[band, to], mback.at[band, ring],
            a2_send.at[band, k - 1], a2_recv.at[band, k - 1], ring_at(k),
        )

    for i in (4, 5, 6, 7):
        loads[i].wait()

    @jax.named_scope("keys_values")
    def keys_values(band, start, count):
        tokens = xall[band, start : start + count].reshape(count * 128, 256)
        for buffer, weight in ((kb, wqkv[1]), (vb, wqkv[2])):
            made = dot(tokens, weight).astype(BF16)
            buffer[band, start : start + count] = made.reshape(count, 8, 16, 256)

    @jax.named_scope("attend")
    def attend(band):
        jobs = [(cell, half) for cell in range(8) for half in range(2)]
        zero = jnp.zeros((64, 128), BF16)

        def doubled(buffer, cell, half):
            rows = buffer[band, 2 * half : 2 * half + 4, cell].reshape(64, 256)
            upper = jnp.concatenate([rows[:, :128], zero], axis=1)
            return jnp.concatenate([upper, jnp.concatenate([zero, rows[:, 128:]], axis=1)], axis=0)

        expos = []
        for cell, half in jobs:
            query = qb[band, 2 * half : 2 * half + 2, cell]
            spread = (query[:, None] * hmask[...][None]).reshape(128, 256)
            scores = lax.dot_general(
                doubled(kb, cell, half), spread, (((1,), (1,)), ((), ())),
                preferred_element_type=F32,
            )
            scores = scores * (1.4426950408889634 * 32**-0.5) + bias[half]
            expos.append(scores.reshape(2, 64, 128))
        expos = [jnp.exp2(e - jnp.max(e, axis=1, keepdims=True)) for e in expos]
        norms = [1.0 / jnp.sum(e, axis=1, keepdims=True) for e in expos]
        head = (iota((2, 16, 256), 2) >> 5) & 3
        for (cell, half), expo, norm in zip(jobs, expos, norms):
            weights = (expo * norm).astype(BF16).reshape(128, 128)
            mixed = lax.dot_general(
                weights, doubled(vb, cell, half), (((0,), (0,)), ((), ())),
                preferred_element_type=F32,
            ).reshape(2, 4, 16, 256)
            own = mixed[:, 0]
            for h in range(1, 4):
                own = jnp.where(head == h, mixed[:, h], own)
            mb[band, 2 * half : 2 * half + 2, 16 * cell : 16 * cell + 16] = own.astype(BF16)

    @pl.loop(0, BANDS + 1)
    def _(i):
        @pl.when(i < BANDS)
        def _():
            with jax.named_scope('a1_wait'):
              for k in (1, 2, 3):
                a1_copy(i, k).wait()
            forward(i).start()

            with jax.named_scope("queries"):
                tokens = xall[i, 2:6].reshape(512, 256)
                qb[i] = dot(tokens, wqkv[0]).astype(BF16).reshape(4, 8, 16, 256)
            keys_values(i, 2, 4)

        @pl.when(i >= 1)
        def _():
            band = i - 1
            with jax.named_scope('fw_wait'):
              forward(band).wait()

            keys_values(band, 0, 2)

            attend(band)
            for k in (1, 2, 3):
                a2_copy(band, k).start()
            mback[band, ring] = mb[band, ring]

    @pl.loop(0, BANDS)
    def _(band):
        with jax.named_scope('a2_wait'):
          for k in (1, 2, 3):
            a2_copy(band, k).wait()
        with jax.named_scope("outproj"):
            total = hidden[band].astype(F32) + dot(mback[band].reshape(512, 256), wo[...])
            res[:, pl.ds(band_column(band), 4)] = total.astype(BF16).reshape(8, 4, 16, 256)

    stores = []
    for half in range(2):
        with jax.named_scope("unperm"):
            for y in range(4 * half, 4 * half + 4):
                o = dot(perm[...], res[y].reshape(256, 256)).astype(BF16)
                ov[:, y] = o.reshape(16, 16, 256)
        rows = pl.ds(4 * half, 4)
        stores.append(
            pltpu.make_async_copy(ov.at[:, rows], out_hbm.at[:, rows], store_sem.at[half])
        )
        stores[half].start()
    with jax.named_scope("store"):
        for store in stores:
            store.wait()


def solution(mesh):
    tm_count = mesh.shape["tm"]

    def step(x, norm_gain, conv_space, conv_time, attn_gain, wq, wk, wv, wo):
        def vmem(*shape, dtype=BF16):
            return pltpu.VMEM(shape, dtype)

        dma = pltpu.SemaphoreType.DMA
        anywhere = pl.BlockSpec(memory_space=pltpu.HBM)
        here = pl.BlockSpec(memory_space=pltpu.VMEM)
        return pl.pallas_call(
            functools.partial(kernel, tm_count),
            out_shape=jax.ShapeDtypeStruct(x.shape, x.dtype),
            in_specs=[
                anywhere, here, anywhere, anywhere, here,
                anywhere, anywhere, anywhere, anywhere,
            ],
            out_specs=anywhere,
            scratch_shapes=[
                vmem(16, 8, 16, 256), vmem(3, 3, 256, 256), vmem(3, 256, 256),
                vmem(3, 256, 256), vmem(256, 256),
                vmem(256, 256), vmem(32, 256), vmem(512, 32), vmem(2, 128, 128, dtype=F32),
                vmem(4, 16, 256),
                vmem(10, 18, 16, 256), vmem(8, 16, 16, 256), vmem(BANDS, 512, 256),
                vmem(BANDS, 2, 32, 256), vmem(BANDS, 2, 32, 256), vmem(BANDS, 512, 256),
                vmem(BANDS, 4, 128, 256), vmem(BANDS, 6, 128, 256),
                vmem(BANDS, 4, 8, 16, 256), vmem(BANDS, 6, 8, 16, 256),
                vmem(BANDS, 6, 8, 16, 256), vmem(BANDS, 4, 128, 256),
                vmem(BANDS, 4, 128, 256), vmem(8, 16, 16, 256), vmem(16, 8, 16, 256),
                dma((8,)), dma((2,)), dma((3,)), dma((3,)), dma((BANDS,)), dma((BANDS,)),
                dma((BANDS, 3)), dma((BANDS, 3)), dma((BANDS,)), dma((BANDS,)),
                dma((BANDS, 3)), dma((BANDS, 3)),
            ],
            compiler_params=pltpu.CompilerParams(
                collective_id=0, has_side_effects=True, vmem_limit_bytes=60 << 20
            ),
            name="encoder_block",
        )(
            x, norm_gain.reshape(1, -1), conv_space, conv_time, attn_gain.reshape(1, -1),
            wq, wk, wv, wo,
        )

    tile = P("tm", "row", "col", None)
    return jax.shard_map(
        step,
        mesh=mesh,
        in_specs=(tile, P(), P(), P(), P(), P(), P(), P(), P()),
        out_specs=tile,
        check_vma=False,
    )
```

```python
import functools

import jax
import jax.numpy as jnp
from jax import lax
from jax.experimental import pallas as pl
from jax.experimental.pallas import tpu as pltpu
from jax.sharding import PartitionSpec as P

RING = 4
BANDS = 4
MESH = pl.DeviceIdType.MESH
F32 = jnp.float32
BF16 = jnp.bfloat16


def dot(a, b):
    return jnp.dot(a, b, preferred_element_type=F32)


def iota(shape, dim):
    return lax.broadcasted_iota(jnp.int32, shape, dim)


def kernel(
    tm_count,
    x_hbm, ng_ref, cs_hbm, ct_hbm, ag_ref, wq_hbm, wk_hbm, wv_hbm, wo_hbm,
    out_hbm,
    xs, cs, ct, wqkv, wo,
    perm, pick, place, bias, hmask,
    ext, xp, sp, hsend, hrecv, hidden, abuf, xall, qb, kb, vb, mb, mback, res, ov,
    load_sem, store_sem, rim_send, rim_recv, th_send, th_recv,
    a1_send, a1_recv, fw_send, fw_recv, a2_send, a2_recv,
):
    tm, row, col = (lax.axis_index(a) for a in ("tm", "row", "col"))
    ring, group = lax.rem(tm, RING), lax.div(tm, RING)
    groups = tm_count // RING

    def ring_at(k):
        return {"tm": group * RING + lax.rem(ring + k, RING)}

    core = {"row": 1 - row}
    side = {"col": 1 - col}
    diag = {"row": 1 - row, "col": 1 - col}
    has_prev, has_next = tm > 0, tm < tm_count - 1
    has_group_prev, has_group_next = group > 0, group < groups - 1
    tm_next, tm_prev = ({"tm": lax.rem(tm + d, tm_count)} for d in (1, tm_count - 1))
    group_next, group_prev = (
        {"tm": lax.rem(group + d, groups) * RING + ring} for d in (1, groups - 1)
    )

    row_halves = (4 * (1 - row), 4 * row)
    loads = [
        pltpu.make_async_copy(src, dst, load_sem.at[i])
        for i, (src, dst) in enumerate(
            [(x_hbm.at[:, pl.ds(y0, 4)], xs.at[:, pl.ds(y0, 4)]) for y0 in row_halves]
            + [
                (cs_hbm, cs), (ct_hbm, ct), (wq_hbm, wqkv.at[0]),
                (wk_hbm, wqkv.at[1]), (wv_hbm, wqkv.at[2]), (wo_hbm, wo),
            ]
        )
    ]
    for load in loads:
        load.start()

    barrier = pltpu.get_barrier_semaphore()
    def greet(partner):
        pl.semaphore_signal(barrier, inc=1, device_id=partner, device_id_type=MESH)

    partners = (core, side, diag, ring_at(1), ring_at(2), ring_at(3))
    for partner in partners:
        greet(partner)
    pl.when(has_prev)(lambda: greet(tm_prev))
    pl.when(has_group_prev)(lambda: greet(group_prev))

    def remote(src, dst, send, recv, where):
        return pltpu.make_async_remote_copy(
            src_ref=src, dst_ref=dst, send_sem=send, recv_sem=recv,
            device_id=where, device_id_type=MESH,
        )

    r, s = iota((256, 256), 0), iota((256, 256), 1)
    perm[...] = (((r >> 4) == (s & 15)) & ((r & 15) == (s >> 4))).astype(F32).astype(BF16)
    r, s = iota((32, 256), 0), iota((32, 256), 1)
    pick[...] = (s == (r & 15) * 16 + 14 + (r >> 4)).astype(F32).astype(BF16)
    r, s = iota((512, 32), 0), iota((512, 32), 1)
    lag, cell, frame = r >> 8, (r >> 4) & 15, r & 15
    hit = (s == (frame + 1 - lag) * 16 + cell) & (frame <= lag) & (tm > 0)
    place[...] = hit.astype(F32).astype(BF16)
    key, lane = iota((128, 128), 0) & 63, iota((128, 128), 1)
    query = (lane & 15) + 16 * (lane >> 6)
    for half in range(2):
        first = jnp.where(group == 0, 32 - 32 * half, 0)
        seen = (key > query) & (key <= query + 32) & (key >= first)
        bias[half] = jnp.where(seen, 0.0, -1e30).astype(F32)
    h, lane = iota((4, 16, 256), 0), iota((4, 16, 256), 2)
    hmask[...] = (h == ((lane >> 5) & 3)).astype(F32).astype(BF16)
    ext[9 * row] = jnp.zeros((18, 16, 256), BF16)
    for y in range(10):
        ext[y, 17 * col] = jnp.zeros((16, 256), BF16)

    @jax.named_scope("norm_rows")
    def norm_rows(half):
        loads[half].wait()
        for i in range(4):
            y = row_halves[half] + i
            v = dot(perm[...], xs[:, y].reshape(256, 256))
            scale = lax.rsqrt(jnp.mean(v * v, axis=-1, keepdims=True) + 1e-6)
            ext[y + 1, pl.ds(1, 16)] = (v * scale * ng_ref[...]).astype(BF16).reshape(16, 16, 256)
            xp[y] = v.astype(BF16).reshape(16, 16, 256)

    @pl.when(tm == 0)
    def _():
        hrecv[...] = jnp.zeros(hrecv.shape, BF16)

    @pl.when(group == 0)
    def _():
        for band in range(BANDS):
            xall[band, 0:2] = jnp.zeros((2, 128, 256), BF16)

    norm_rows(0)
    with jax.named_scope("barrier"):
        later = has_next.astype(jnp.int32) + has_group_next.astype(jnp.int32)
        pl.semaphore_wait(barrier, len(partners) + later)
    rim_y, rim_x = 8 - 7 * row, 16 - 15 * col
    rims = [
        remote(
            ext.at[rim_y, pl.ds(1, 16)], ext.at[9 * row, pl.ds(1, 16)],
            rim_send.at[0], rim_recv.at[0], core,
        ),
        remote(
            ext.at[rim_y, rim_x], ext.at[9 * row, 17 * col],
            rim_send.at[1], rim_recv.at[1], diag,
        ),
        remote(
            ext.at[pl.ds(1, 8), rim_x], ext.at[pl.ds(1, 8), 17 * col],
            rim_send.at[2], rim_recv.at[2], side,
        ),
    ]
    rims[0].start()
    rims[1].start()

    norm_rows(1)
    rims[2].start()
    loads[2].wait()
    loads[3].wait()

    def band_column(band):
        return 4 * band + col * (12 - 8 * band)

    @jax.named_scope("conv")
    def conv(band):
        c0 = band_column(band)
        total = None
        for dy in range(3):
            for dx in range(3):
                cells = ext[dy : dy + 8, pl.ds(c0 + dx, 4)].reshape(512, 256)
                term = dot(cells, cs[dy, dx])
                total = term if total is None else total + term
        act = (0.5 * total * (1.0 + jnp.tanh(0.5 * total))).astype(BF16)
        sp[band] = act
        for half in range(2):
            last = dot(pick[...], act[256 * half : 256 * half + 256])
            hsend[band, half] = last.astype(BF16)

    def tm_copy(band):
        return remote(
            hsend.at[band], hrecv.at[band], th_send.at[band], th_recv.at[band], tm_next
        )

    @jax.named_scope("temporal")
    def temporal(band):
        act = sp[band]
        wide = act.astype(F32).reshape(32, 16, 256)
        early = [dot(place[...], hrecv[band, half]) for half in range(2)]
        frame = iota((32, 16, 256), 1)
        total = dot(act, ct[0])
        for lag in (1, 2):
            before = [e[256 * (lag - 1) : 256 * lag] for e in early]
            before = jnp.concatenate(before, axis=0).reshape(32, 16, 256)
            moved = jnp.where(frame < lag, before, pltpu.roll(wide, lag, 1))
            total = total + dot(moved.astype(BF16).reshape(512, 256), ct[lag])
        own = xp[:, pl.ds(band_column(band), 4)].reshape(512, 256).astype(F32)
        hid = (own + total).astype(BF16)
        hidden[band] = hid
        v = hid.astype(F32)
        scale = lax.rsqrt(jnp.mean(v * v, axis=-1, keepdims=True) + 1e-6)
        abuf[band] = (v * scale * ag_ref[...]).astype(BF16).reshape(4, 128, 256)

    def a1_copy(band, k):
        to = lax.rem(ring + k, RING)
        return remote(
            abuf.at[band, to], xall.at[band, 2 + ring],
            a1_send.at[band, k - 1], a1_recv.at[band, k - 1], ring_at(k),
        )

    @pl.loop(0, BANDS)
    def _(band):
        @pl.when(band == 0)
        @jax.named_scope("rim_wait")
        def _():
            rims[0].wait()

        @pl.when(band == BANDS - 1)
        @jax.named_scope("rim_wait2")
        def _():
            rims[1].wait()
            rims[2].wait()

        conv(band)
        pl.when(has_next)(lambda: tm_copy(band).start())

    @pl.loop(0, BANDS)
    def _(band):
        with jax.named_scope("tm_wait"):
            pl.when(has_prev)(lambda: tm_copy(band).wait_recv())
        temporal(band)
        for k in (1, 2, 3):
            a1_copy(band, k).start()
        xall[band, 2 + ring] = abuf[band, ring]

    def forward(band):
        return remote(
            xall.at[band, pl.ds(4, 2)], xall.at[band, pl.ds(0, 2)],
            fw_send.at[band], fw_recv.at[band], group_next,
        )

    def a2_copy(band, k):
        to = lax.rem(ring + k, RING)
        return remote(
            mb.at[band, to], mback.at[band, ring],
            a2_send.at[band, k - 1], a2_recv.at[band, k - 1], ring_at(k),
        )

    for i in (4, 5, 6, 7):
        loads[i].wait()

    @jax.named_scope("keys_values")
    def keys_values(band, start, count):
        tokens = xall[band, start : start + count].reshape(count * 128, 256)
        for buffer, weight in ((kb, wqkv[1]), (vb, wqkv[2])):
            made = dot(tokens, weight).astype(BF16)
            buffer[band, start : start + count] = made.reshape(count, 8, 16, 256)

    @jax.named_scope("attend")
    def attend(band):
        jobs = [(cell, half) for cell in range(8) for half in range(2)]
        zero = jnp.zeros((64, 128), BF16)

        def doubled(buffer, cell, half):
            rows = buffer[band, 2 * half : 2 * half + 4, cell].reshape(64, 256)
            upper = jnp.concatenate([rows[:, :128], zero], axis=1)
            return jnp.concatenate([upper, jnp.concatenate([zero, rows[:, 128:]], axis=1)], axis=0)

        expos = []
        for cell, half in jobs:
            query = qb[band, 2 * half : 2 * half + 2, cell]
            spread = (query[:, None] * hmask[...][None]).reshape(128, 256)
            scores = lax.dot_general(
                doubled(kb, cell, half), spread, (((1,), (1,)), ((), ())),
                preferred_element_type=F32,
            )
            scores = scores * (1.4426950408889634 * 32**-0.5) + bias[half]
            expos.append(scores.reshape(2, 64, 128))
        expos = [jnp.exp2(e - jnp.max(e, axis=1, keepdims=True)) for e in expos]
        norms = [1.0 / jnp.sum(e, axis=1, keepdims=True) for e in expos]
        head = (iota((2, 16, 256), 2) >> 5) & 3
        for (cell, half), expo, norm in zip(jobs, expos, norms):
            weights = (expo * norm).astype(BF16).reshape(128, 128)
            mixed = lax.dot_general(
                weights, doubled(vb, cell, half), (((0,), (0,)), ((), ())),
                preferred_element_type=F32,
            ).reshape(2, 4, 16, 256)
            own = mixed[:, 0]
            for h in range(1, 4):
                own = jnp.where(head == h, mixed[:, h], own)
            mb[band, 2 * half : 2 * half + 2, 16 * cell : 16 * cell + 16] = own.astype(BF16)

    @pl.loop(0, BANDS + 1)
    def _(i):
        @pl.when(i < BANDS)
        def _():
            with jax.named_scope('a1_wait'):
              for k in (1, 2, 3):
                a1_copy(i, k).wait()
            pl.when(has_group_next)(lambda: forward(i).start())

            with jax.named_scope("queries"):
                tokens = xall[i, 2:6].reshape(512, 256)
                qb[i] = dot(tokens, wqkv[0]).astype(BF16).reshape(4, 8, 16, 256)
            keys_values(i, 2, 4)

        @pl.when(i >= 1)
        def _():
            band = i - 1
            with jax.named_scope('fw_wait'):
              pl.when(has_group_prev)(lambda: forward(band).wait_recv())

            keys_values(band, 0, 2)

            attend(band)
            for k in (1, 2, 3):
                a2_copy(band, k).start()
            mback[band, ring] = mb[band, ring]

    @pl.loop(0, BANDS)
    def _(band):
        with jax.named_scope('a2_wait'):
          for k in (1, 2, 3):
            a2_copy(band, k).wait()
        with jax.named_scope("outproj"):
            total = hidden[band].astype(F32) + dot(mback[band].reshape(512, 256), wo[...])
            res[:, pl.ds(band_column(band), 4)] = total.astype(BF16).reshape(8, 4, 16, 256)

    stores = []
    for half in range(2):
        with jax.named_scope("unperm"):
            for y in range(4 * half, 4 * half + 4):
                o = dot(perm[...], res[y].reshape(256, 256)).astype(BF16)
                ov[:, y] = o.reshape(16, 16, 256)
        rows = pl.ds(4 * half, 4)
        stores.append(
            pltpu.make_async_copy(ov.at[:, rows], out_hbm.at[:, rows], store_sem.at[half])
        )
        stores[half].start()
    @pl.loop(0, BANDS)
    def _(band):
        pl.when(has_next)(lambda: tm_copy(band).wait_send())
        pl.when(has_group_next)(lambda: forward(band).wait_send())

    with jax.named_scope("store"):
        for store in stores:
            store.wait()


def solution(mesh):
    tm_count = mesh.shape["tm"]

    def step(x, norm_gain, conv_space, conv_time, attn_gain, wq, wk, wv, wo):
        def vmem(*shape, dtype=BF16):
            return pltpu.VMEM(shape, dtype)

        dma = pltpu.SemaphoreType.DMA
        anywhere = pl.BlockSpec(memory_space=pltpu.HBM)
        here = pl.BlockSpec(memory_space=pltpu.VMEM)
        return pl.pallas_call(
            functools.partial(kernel, tm_count),
            out_shape=jax.ShapeDtypeStruct(x.shape, x.dtype),
            in_specs=[
                anywhere, here, anywhere, anywhere, here,
                anywhere, anywhere, anywhere, anywhere,
            ],
            out_specs=anywhere,
            scratch_shapes=[
                vmem(16, 8, 16, 256), vmem(3, 3, 256, 256), vmem(3, 256, 256),
                vmem(3, 256, 256), vmem(256, 256),
                vmem(256, 256), vmem(32, 256), vmem(512, 32), vmem(2, 128, 128, dtype=F32),
                vmem(4, 16, 256),
                vmem(10, 18, 16, 256), vmem(8, 16, 16, 256), vmem(BANDS, 512, 256),
                vmem(BANDS, 2, 32, 256), vmem(BANDS, 2, 32, 256), vmem(BANDS, 512, 256),
                vmem(BANDS, 4, 128, 256), vmem(BANDS, 6, 128, 256),
                vmem(BANDS, 4, 8, 16, 256), vmem(BANDS, 6, 8, 16, 256),
                vmem(BANDS, 6, 8, 16, 256), vmem(BANDS, 4, 128, 256),
                vmem(BANDS, 4, 128, 256), vmem(8, 16, 16, 256), vmem(16, 8, 16, 256),
                dma((8,)), dma((2,)), dma((3,)), dma((3,)), dma((BANDS,)), dma((BANDS,)),
                dma((BANDS, 3)), dma((BANDS, 3)), dma((BANDS,)), dma((BANDS,)),
                dma((BANDS, 3)), dma((BANDS, 3)),
            ],
            compiler_params=pltpu.CompilerParams(
                collective_id=0, has_side_effects=True, vmem_limit_bytes=60 << 20
            ),
            name="encoder_block",
        )(
            x, norm_gain.reshape(1, -1), conv_space, conv_time, attn_gain.reshape(1, -1),
            wq, wk, wv, wo,
        )

    tile = P("tm", "row", "col", None)
    return jax.shard_map(
        step,
        mesh=mesh,
        in_specs=(tile, P(), P(), P(), P(), P(), P(), P(), P()),
        out_specs=tile,
        check_vma=False,
    )
```

```python
import functools

import jax
import jax.numpy as jnp
from jax import lax
from jax.experimental import pallas as pl
from jax.experimental.pallas import tpu as pltpu
from jax.sharding import PartitionSpec as P

RING = 4
BANDS = 4
MESH = pl.DeviceIdType.MESH
F32 = jnp.float32
BF16 = jnp.bfloat16


def dot(a, b):
    return jnp.dot(a, b, preferred_element_type=F32)


def iota(shape, dim):
    return lax.broadcasted_iota(jnp.int32, shape, dim)


def kernel(
    tm_count,
    x_hbm, ng_ref, cs_hbm, ct_hbm, ag_ref, wq_hbm, wk_hbm, wv_hbm, wo_hbm,
    out_hbm,
    xs, cs, ct, wqkv, wo,
    perm, pick, place, bias, hmask,
    ext, xp, sp, hsend, hrecv, hidden, abuf, xall, qb, kb, vb, mb, mback, res, ov,
    load_sem, store_sem, rim_send, rim_recv, th_send, th_recv,
    a1_send, a1_recv, fw_send, fw_recv, a2_send, a2_recv,
):
    tm, row, col = (lax.axis_index(a) for a in ("tm", "row", "col"))
    ring, group = lax.rem(tm, RING), lax.div(tm, RING)
    groups = tm_count // RING

    def ring_at(k):
        return {"tm": group * RING + lax.rem(ring + k, RING)}

    core = {"row": 1 - row}
    side = {"col": 1 - col}
    diag = {"row": 1 - row, "col": 1 - col}
    has_prev, has_next = tm > 0, tm < tm_count - 1
    has_group_prev, has_group_next = group > 0, group < groups - 1
    tm_next, tm_prev = ({"tm": lax.rem(tm + d, tm_count)} for d in (1, tm_count - 1))
    group_next, group_prev = (
        {"tm": lax.rem(group + d, groups) * RING + ring} for d in (1, groups - 1)
    )

    row_halves = (4 * (1 - row), 4 * row)
    loads = [
        pltpu.make_async_copy(src, dst, load_sem.at[i])
        for i, (src, dst) in enumerate(
            [(x_hbm.at[:, y0 + k], xs.at[:, y0 + k]) for y0 in row_halves for k in range(4)]
            + [
                (cs_hbm, cs), (ct_hbm, ct), (wq_hbm, wqkv.at[0]),
                (wk_hbm, wqkv.at[1]), (wv_hbm, wqkv.at[2]), (wo_hbm, wo),
            ]
        )
    ]
    for load in loads:
        load.start()

    barrier = pltpu.get_barrier_semaphore()
    def greet(partner):
        pl.semaphore_signal(barrier, inc=1, device_id=partner, device_id_type=MESH)

    partners = (core, side, diag, ring_at(1), ring_at(2), ring_at(3))
    for partner in partners:
        greet(partner)
    pl.when(has_prev)(lambda: greet(tm_prev))
    pl.when(has_group_prev)(lambda: greet(group_prev))

    def remote(src, dst, send, recv, where):
        return pltpu.make_async_remote_copy(
            src_ref=src, dst_ref=dst, send_sem=send, recv_sem=recv,
            device_id=where, device_id_type=MESH,
        )

    r, s = iota((256, 256), 0), iota((256, 256), 1)
    perm[...] = (((r >> 4) == (s & 15)) & ((r & 15) == (s >> 4))).astype(F32).astype(BF16)
    r, s = iota((32, 256), 0), iota((32, 256), 1)
    pick[...] = (s == (r & 15) * 16 + 14 + (r >> 4)).astype(F32).astype(BF16)
    r, s = iota((512, 32), 0), iota((512, 32), 1)
    lag, cell, frame = r >> 8, (r >> 4) & 15, r & 15
    hit = (s == (frame + 1 - lag) * 16 + cell) & (frame <= lag) & (tm > 0)
    place[...] = hit.astype(F32).astype(BF16)
    key, lane = iota((128, 128), 0) & 63, iota((128, 128), 1)
    query = (lane & 15) + 16 * (lane >> 6)
    for half in range(2):
        first = jnp.where(group == 0, 32 - 32 * half, 0)
        seen = (key > query) & (key <= query + 32) & (key >= first)
        bias[half] = jnp.where(seen, 0.0, -1e30).astype(F32)
    h, lane = iota((4, 16, 256), 0), iota((4, 16, 256), 2)
    hmask[...] = (h == ((lane >> 5) & 3)).astype(F32).astype(BF16)
    ext[9 * row] = jnp.zeros((18, 16, 256), BF16)
    for y in range(10):
        ext[y, 17 * col] = jnp.zeros((16, 256), BF16)

    @jax.named_scope("norm_rows")
    def norm_rows(half):
        for i in range(4):
            loads[4 * half + i].wait()
        for i in range(4):
            y = row_halves[half] + i
            v = dot(perm[...], xs[:, y].reshape(256, 256))
            scale = lax.rsqrt(jnp.mean(v * v, axis=-1, keepdims=True) + 1e-6)
            ext[y + 1, pl.ds(1, 16)] = (v * scale * ng_ref[...]).astype(BF16).reshape(16, 16, 256)
            xp[y] = v.astype(BF16).reshape(16, 16, 256)

    @pl.when(tm == 0)
    def _():
        hrecv[...] = jnp.zeros(hrecv.shape, BF16)

    @pl.when(group == 0)
    def _():
        for band in range(BANDS):
            xall[band, 0:2] = jnp.zeros((2, 128, 256), BF16)

    norm_rows(0)
    with jax.named_scope("barrier"):
        later = has_next.astype(jnp.int32) + has_group_next.astype(jnp.int32)
        pl.semaphore_wait(barrier, len(partners) + later)
    rim_y, rim_x = 8 - 7 * row, 16 - 15 * col
    rims = [
        remote(
            ext.at[rim_y, pl.ds(1, 16)], ext.at[9 * row, pl.ds(1, 16)],
            rim_send.at[0], rim_recv.at[0], core,
        ),
        remote(
            ext.at[rim_y, rim_x], ext.at[9 * row, 17 * col],
            rim_send.at[1], rim_recv.at[1], diag,
        ),
        remote(
            ext.at[pl.ds(1, 8), rim_x], ext.at[pl.ds(1, 8), 17 * col],
            rim_send.at[2], rim_recv.at[2], side,
        ),
    ]
    rims[0].start()
    rims[1].start()

    norm_rows(1)
    rims[2].start()
    loads[8].wait()
    loads[9].wait()

    def corner(band):
        return 4 * ((row + band) & 1), 8 * ((col + (band >> 1)) & 1)

    @jax.named_scope("conv")
    def conv(band):
        y0, c0 = corner(band)
        total = None
        for dy in range(3):
            for dx in range(3):
                cells = ext[pl.ds(y0 + dy, 4), pl.ds(c0 + dx, 8)].reshape(512, 256)
                term = dot(cells, cs[dy, dx])
                total = term if total is None else total + term
        act = (0.5 * total * (1.0 + jnp.tanh(0.5 * total))).astype(BF16)
        sp[band] = act
        for half in range(2):
            last = dot(pick[...], act[256 * half : 256 * half + 256])
            hsend[band, half] = last.astype(BF16)

    def tm_copy(band):
        return remote(
            hsend.at[band], hrecv.at[band], th_send.at[band], th_recv.at[band], tm_next
        )

    def shares(buffer, band, tokens):
        tokens = tokens.reshape(4, 8, 16, 256)
        for q in range(RING):
            buffer[band, q] = tokens[:, 2 * q : 2 * q + 2].reshape(128, 256)

    @jax.named_scope("temporal")
    def temporal(band):
        act = sp[band]
        wide = act.astype(F32).reshape(32, 16, 256)
        early = [dot(place[...], hrecv[band, half]) for half in range(2)]
        frame = iota((32, 16, 256), 1)
        total = dot(act, ct[0])
        for lag in (1, 2):
            before = [e[256 * (lag - 1) : 256 * lag] for e in early]
            before = jnp.concatenate(before, axis=0).reshape(32, 16, 256)
            moved = jnp.where(frame < lag, before, pltpu.roll(wide, lag, 1))
            total = total + dot(moved.astype(BF16).reshape(512, 256), ct[lag])
        y0, c0 = corner(band)
        own = xp[pl.ds(y0, 4), pl.ds(c0, 8)].reshape(512, 256).astype(F32)
        hid = (own + total).astype(BF16)
        shares(hidden, band, hid)
        v = hid.astype(F32)
        scale = lax.rsqrt(jnp.mean(v * v, axis=-1, keepdims=True) + 1e-6)
        shares(abuf, band, (v * scale * ag_ref[...]).astype(BF16))

    def a1_copy(band, k):
        to = lax.rem(ring + k, RING)
        return remote(
            abuf.at[band, to], xall.at[band, 2 + ring],
            a1_send.at[band, k - 1], a1_recv.at[band, k - 1], ring_at(k),
        )

    @pl.loop(0, BANDS)
    def _(band):
        for step, rim in ((1, 0), (2, 2), (3, 1)):
            pl.when(band == step)(lambda rim=rim: rims[rim].wait())

        conv(band)
        pl.when(has_next)(lambda: tm_copy(band).start())

    def forward(band, part):
        return remote(
            xall.at[band, 4 + part], xall.at[band, part],
            fw_send.at[band, part], fw_recv.at[band, part], group_next,
        )

    @pl.loop(0, BANDS)
    def _(band):
        with jax.named_scope("tm_wait"):
            pl.when(has_prev)(lambda: tm_copy(band).wait_recv())
        temporal(band)
        for k in (1, 2, 3):
            a1_copy(band, k).start()
        xall[band, 2 + ring] = abuf[band, ring]
        for part in (0, 1):
            pl.when(has_group_next & (ring == part + 2))(
                lambda part=part: forward(band, part).start()
            )

    def a2_copy(band, k):
        to = lax.rem(ring + k, RING)
        return remote(
            mb.at[band, to], mback.at[band, ring],
            a2_send.at[band, k - 1], a2_recv.at[band, k - 1], ring_at(k),
        )

    for i in (10, 11, 12, 13):
        loads[i].wait()

    @jax.named_scope("keys_values")
    def keys_values(band, start, count):
        tokens = xall[band, start : start + count].reshape(count * 128, 256)
        for buffer, weight in ((kb, wqkv[1]), (vb, wqkv[2])):
            made = dot(tokens, weight).astype(BF16)
            buffer[band, start : start + count] = made.reshape(count, 8, 16, 256)

    @jax.named_scope("attend")
    def attend(band, half):
        jobs = [(cell, half) for cell in range(8)]
        zero = jnp.zeros((64, 128), BF16)

        def doubled(buffer, cell, half):
            rows = buffer[band, 2 * half : 2 * half + 4, cell].reshape(64, 256)
            upper = jnp.concatenate([rows[:, :128], zero], axis=1)
            return jnp.concatenate([upper, jnp.concatenate([zero, rows[:, 128:]], axis=1)], axis=0)

        expos = []
        for cell, half in jobs:
            query = qb[band, 2 * half : 2 * half + 2, cell]
            spread = (query[:, None] * hmask[...][None]).reshape(128, 256)
            scores = lax.dot_general(
                doubled(kb, cell, half), spread, (((1,), (1,)), ((), ())),
                preferred_element_type=F32,
            )
            scores = scores * (1.4426950408889634 * 32**-0.5) + bias[half]
            expos.append(scores.reshape(2, 64, 128))
        expos = [jnp.exp2(e - jnp.max(e, axis=1, keepdims=True)) for e in expos]
        norms = [1.0 / jnp.sum(e, axis=1, keepdims=True) for e in expos]
        head = (iota((2, 16, 256), 2) >> 5) & 3
        for (cell, half), expo, norm in zip(jobs, expos, norms):
            weights = (expo * norm).astype(BF16).reshape(128, 128)
            mixed = lax.dot_general(
                weights, doubled(vb, cell, half), (((0,), (0,)), ((), ())),
                preferred_element_type=F32,
            ).reshape(2, 4, 16, 256)
            own = mixed[:, 0]
            for h in range(1, 4):
                own = jnp.where(head == h, mixed[:, h], own)
            mb[band, 2 * half : 2 * half + 2, 16 * cell : 16 * cell + 16] = own.astype(BF16)

    def send_back(band, half):
        for k in (1, 2, 3):
            to = lax.rem(ring + k, RING)
            pl.when(lax.div(to, 2) == half)(lambda k=k: a2_copy(band, k).start())

        @pl.when(lax.div(ring, 2) == half)
        def _():
            mback[band, ring] = mb[band, ring]

    @jax.named_scope("a1_wait")
    def arrive(band, source):
        k = lax.rem(ring + RING - source, RING)

        @pl.when(k > 0)
        def _():
            a1_copy(band, k).wait_recv()
            if source >= 2:
                pl.when(has_group_next)(lambda: forward(band, source - 2).start())

    arrive(0, 3)
    arrive(0, 2)

    @pl.loop(0, BANDS + 1)
    def _(i):
        @pl.when(i < BANDS)
        def _():
            arrive(i, 1)
            arrive(i, 0)
            with jax.named_scope("queries"):
                tokens = xall[i, 2:6].reshape(512, 256)
                qb[i] = dot(tokens, wqkv[0]).astype(BF16).reshape(4, 8, 16, 256)
            keys_values(i, 2, 4)
            attend(i, 1)
            send_back(i, 1)

        @pl.when(i < BANDS - 1)
        def _():
            arrive(i + 1, 3)
            arrive(i + 1, 2)

        @pl.when(i >= 1)
        def _():
            band = i - 1
            with jax.named_scope("fw_wait"):
                for part in (0, 1):
                    pl.when(has_group_prev)(lambda part=part: forward(band, part).wait_recv())
            keys_values(band, 0, 2)
            attend(band, 0)
            send_back(band, 0)

    @pl.loop(0, BANDS)
    def _(band):
        with jax.named_scope('a2_wait'):
          for k in (1, 2, 3):
            a2_copy(band, k).wait()
        y0, c0 = corner(band)
        with jax.named_scope("outproj"):
            total = dot(mback[band].reshape(512, 256), wo[...])
            total = total + hidden[band].reshape(512, 256).astype(F32)
            total = total.astype(BF16).reshape(RING, 4, 2, 16, 256)
            for q in range(RING):
                res[pl.ds(y0, 4), pl.ds(c0 + 2 * q, 2)] = total[q]

    stores = []
    for half in range(2):
        with jax.named_scope("unperm"):
            for y in range(4 * half, 4 * half + 4):
                o = dot(perm[...], res[y].reshape(256, 256)).astype(BF16)
                ov[:, y] = o.reshape(16, 16, 256)
        rows = pl.ds(4 * half, 4)
        stores.append(
            pltpu.make_async_copy(ov.at[:, rows], out_hbm.at[:, rows], store_sem.at[half])
        )
        stores[half].start()
    @pl.loop(0, BANDS)
    def _(band):
        pl.when(has_next)(lambda: tm_copy(band).wait_send())
        for part in (0, 1):
            pl.when(has_group_next)(lambda part=part: forward(band, part).wait_send())
        for k in (1, 2, 3):
            a1_copy(band, k).wait_send()

    with jax.named_scope("store"):
        for store in stores:
            store.wait()


def solution(mesh):
    tm_count = mesh.shape["tm"]

    def step(x, norm_gain, conv_space, conv_time, attn_gain, wq, wk, wv, wo):
        def vmem(*shape, dtype=BF16):
            return pltpu.VMEM(shape, dtype)

        dma = pltpu.SemaphoreType.DMA
        anywhere = pl.BlockSpec(memory_space=pltpu.HBM)
        here = pl.BlockSpec(memory_space=pltpu.VMEM)
        return pl.pallas_call(
            functools.partial(kernel, tm_count),
            out_shape=jax.ShapeDtypeStruct(x.shape, x.dtype),
            in_specs=[
                anywhere, here, anywhere, anywhere, here,
                anywhere, anywhere, anywhere, anywhere,
            ],
            out_specs=anywhere,
            scratch_shapes=[
                vmem(16, 8, 16, 256), vmem(3, 3, 256, 256), vmem(3, 256, 256),
                vmem(3, 256, 256), vmem(256, 256),
                vmem(256, 256), vmem(32, 256), vmem(512, 32), vmem(2, 128, 128, dtype=F32),
                vmem(4, 16, 256),
                vmem(10, 18, 16, 256), vmem(8, 16, 16, 256), vmem(BANDS, 512, 256),
                vmem(BANDS, 2, 32, 256), vmem(BANDS, 2, 32, 256), vmem(BANDS, 4, 128, 256),
                vmem(BANDS, 4, 128, 256), vmem(BANDS, 6, 128, 256),
                vmem(BANDS, 4, 8, 16, 256), vmem(BANDS, 6, 8, 16, 256),
                vmem(BANDS, 6, 8, 16, 256), vmem(BANDS, 4, 128, 256),
                vmem(BANDS, 4, 128, 256), vmem(8, 16, 16, 256), vmem(16, 8, 16, 256),
                dma((14,)), dma((2,)), dma((3,)), dma((3,)), dma((BANDS,)), dma((BANDS,)),
                dma((BANDS, 3)), dma((BANDS, 3)), dma((BANDS, 2)), dma((BANDS, 2)),
                dma((BANDS, 3)), dma((BANDS, 3)),
            ],
            compiler_params=pltpu.CompilerParams(
                collective_id=0, has_side_effects=True, vmem_limit_bytes=60 << 20
            ),
            name="encoder_block",
        )(
            x, norm_gain.reshape(1, -1), conv_space, conv_time, attn_gain.reshape(1, -1),
            wq, wk, wv, wo,
        )

    tile = P("tm", "row", "col", None)
    return jax.shard_map(
        step,
        mesh=mesh,
        in_specs=(tile, P(), P(), P(), P(), P(), P(), P(), P()),
        out_specs=tile,
        check_vma=False,
    )
```

```python
import functools

import jax
import jax.numpy as jnp
from jax import lax
from jax.experimental import pallas as pl
from jax.experimental.pallas import tpu as pltpu
from jax.sharding import PartitionSpec as P

RING = 4
BANDS = 4
LAG = 2
MESH = pl.DeviceIdType.MESH
F32 = jnp.float32
BF16 = jnp.bfloat16


def dot(a, b):
    return jnp.dot(a, b, preferred_element_type=F32)


def iota(shape, dim):
    return lax.broadcasted_iota(jnp.int32, shape, dim)


def swap():
    r, s = iota((256, 256), 0), iota((256, 256), 1)
    return (((r >> 4) == (s & 15)) & ((r & 15) == (s >> 4))).astype(F32).astype(BF16)


def kernel(
    tm_count,
    x_hbm, ng_ref, cs_hbm, ct_hbm, ag_ref, wq_hbm, wk_hbm, wv_hbm, wo_hbm,
    out_hbm,
    xs, cs, ct, wqkv, wo,
    perm, pick, place, bias, hmask,
    ext, xp, sp, hsend, hrecv, hidden, abuf, xall, qb, kb, vb, mb, mback, res,
    load_sem, store_sem, rim_send, rim_recv, th_send, th_recv,
    a1_send, a1_recv, fw_send, fw_recv, a2_send, a2_recv,
):
    tm, row, col = (lax.axis_index(a) for a in ("tm", "row", "col"))
    ring, group = lax.rem(tm, RING), lax.div(tm, RING)
    groups = tm_count // RING

    def ring_at(k):
        return {"tm": group * RING + lax.rem(ring + k, RING)}

    core = {"row": 1 - row}
    side = {"col": 1 - col}
    diag = {"row": 1 - row, "col": 1 - col}
    has_prev, has_next = tm > 0, tm < tm_count - 1
    has_group_prev, has_group_next = group > 0, group < groups - 1
    tm_next, tm_prev = ({"tm": lax.rem(tm + d, tm_count)} for d in (1, tm_count - 1))
    group_next, group_prev = (
        {"tm": lax.rem(group + d, groups) * RING + ring} for d in (1, groups - 1)
    )

    row_halves = (4 * (1 - row), 4 * row)
    loads = [
        pltpu.make_async_copy(src, dst, load_sem.at[i])
        for i, (src, dst) in enumerate(
            [(x_hbm.at[:, y0 + k], xs.at[:, y0 + k]) for y0 in row_halves for k in range(4)]
            + [
                (cs_hbm, cs), (ct_hbm, ct), (wq_hbm, wqkv.at[0]),
                (wk_hbm, wqkv.at[1]), (wv_hbm, wqkv.at[2]), (wo_hbm, wo),
            ]
        )
    ]
    for load in loads:
        load.start()

    barrier = pltpu.get_barrier_semaphore()
    def greet(partner):
        pl.semaphore_signal(barrier, inc=1, device_id=partner, device_id_type=MESH)

    partners = (core, side, diag, ring_at(1), ring_at(2), ring_at(3))
    for partner in partners:
        greet(partner)
    pl.when(has_prev)(lambda: greet(tm_prev))
    pl.when(has_group_prev)(lambda: greet(group_prev))

    def remote(src, dst, send, recv, where):
        return pltpu.make_async_remote_copy(
            src_ref=src, dst_ref=dst, send_sem=send, recv_sem=recv,
            device_id=where, device_id_type=MESH,
        )

    perm[...] = swap()
    r, s = iota((32, 256), 0), iota((32, 256), 1)
    pick[...] = (s == (r & 15) * 16 + 14 + (r >> 4)).astype(F32).astype(BF16)
    r, s = iota((512, 32), 0), iota((512, 32), 1)
    lag, cell, frame = r >> 8, (r >> 4) & 15, r & 15
    hit = (s == (frame + 1 - lag) * 16 + cell) & (frame <= lag) & (tm > 0)
    place[...] = hit.astype(F32).astype(BF16)
    key, lane = iota((128, 128), 0) & 63, iota((128, 128), 1)
    query = (lane & 15) + 16 * (lane >> 6)
    for half in range(2):
        first = jnp.where(group == 0, 32 - 32 * half, 0)
        seen = (key > query) & (key <= query + 32) & (key >= first)
        bias[half] = jnp.where(seen, 0.0, -1e30).astype(F32)
    h, lane = iota((4, 16, 256), 0), iota((4, 16, 256), 2)
    hmask[...] = (h == ((lane >> 5) & 3)).astype(F32).astype(BF16)
    ext[9 * row] = jnp.zeros((18, 16, 256), BF16)
    for y in range(10):
        ext[y, 17 * col] = jnp.zeros((16, 256), BF16)

    @jax.named_scope("norm_rows")
    def norm_rows(half):
        for i in range(4):
            loads[4 * half + i].wait()
        for i in range(4):
            y = row_halves[half] + i
            v = dot(perm[...], xs[:, y].reshape(256, 256))
            scale = lax.rsqrt(jnp.mean(v * v, axis=-1, keepdims=True) + 1e-6)
            ext[y + 1, pl.ds(1, 16)] = (v * scale * ng_ref[...]).astype(BF16).reshape(16, 16, 256)
            xp[y] = v.astype(BF16).reshape(16, 16, 256)

    @pl.when(tm == 0)
    def _():
        hrecv[...] = jnp.zeros(hrecv.shape, BF16)

    @pl.when(group == 0)
    def _():
        for band in range(BANDS):
            xall[band, 0:2] = jnp.zeros((2, 128, 256), BF16)

    norm_rows(0)
    with jax.named_scope("barrier"):
        later = has_next.astype(jnp.int32) + has_group_next.astype(jnp.int32)
        pl.semaphore_wait(barrier, len(partners) + later)
    rim_y, rim_x = 8 - 7 * row, 16 - 15 * col
    rims = [
        remote(
            ext.at[rim_y, pl.ds(1, 16)], ext.at[9 * row, pl.ds(1, 16)],
            rim_send.at[0], rim_recv.at[0], core,
        ),
        remote(
            ext.at[rim_y, rim_x], ext.at[9 * row, 17 * col],
            rim_send.at[1], rim_recv.at[1], diag,
        ),
    ] + [
        remote(
            ext.at[pl.ds(first, rows), rim_x], ext.at[pl.ds(first, rows), 17 * col],
            rim_send.at[i], rim_recv.at[i], side,
        )
        for i, first, rows in ((2, 1 + 3 * row, 5), (3, 6 - 5 * row, 3))
    ]
    rims[0].start()
    rims[1].start()

    norm_rows(1)
    rims[2].start()
    rims[3].start()
    loads[8].wait()
    loads[9].wait()

    def corner(band):
        return 4 * ((row + band) & 1), 8 * ((col + (band >> 1)) & 1)

    @jax.named_scope("conv")
    def conv(band):
        y0, c0 = corner(band)
        total = None
        for dy in range(3):
            for dx in range(3):
                cells = ext[pl.ds(y0 + dy, 4), pl.ds(c0 + dx, 8)].reshape(512, 256)
                term = dot(cells, cs[dy, dx])
                total = term if total is None else total + term
        act = (0.5 * total * (1.0 + jnp.tanh(0.5 * total))).astype(BF16)
        sp[band] = act
        for half in range(2):
            last = dot(pick[...], act[256 * half : 256 * half + 256])
            hsend[band, half] = last.astype(BF16)

    def tm_copy(band):
        return remote(
            hsend.at[band], hrecv.at[band], th_send.at[band], th_recv.at[band], tm_next
        )

    def shares(buffer, band, tokens):
        tokens = tokens.reshape(4, 8, 16, 256)
        for q in range(RING):
            buffer[band, q] = tokens[:, 2 * q : 2 * q + 2].reshape(128, 256)

    @jax.named_scope("temporal")
    def temporal(band):
        act = sp[band]
        wide = act.astype(F32).reshape(32, 16, 256)
        early = [dot(place[...], hrecv[band, half]) for half in range(2)]
        frame = iota((32, 16, 256), 1)
        total = dot(act, ct[0])
        for lag in (1, 2):
            before = [e[256 * (lag - 1) : 256 * lag] for e in early]
            before = jnp.concatenate(before, axis=0).reshape(32, 16, 256)
            moved = jnp.where(frame < lag, before, pltpu.roll(wide, lag, 1))
            total = total + dot(moved.astype(BF16).reshape(512, 256), ct[lag])
        y0, c0 = corner(band)
        own = xp[pl.ds(y0, 4), pl.ds(c0, 8)].reshape(512, 256).astype(F32)
        hid = (own + total).astype(BF16)
        shares(hidden, band, hid)
        v = hid.astype(F32)
        scale = lax.rsqrt(jnp.mean(v * v, axis=-1, keepdims=True) + 1e-6)
        shares(abuf, band, (v * scale * ag_ref[...]).astype(BF16))

    def a1_copy(band, k):
        to = lax.rem(ring + k, RING)
        return remote(
            abuf.at[band, to], xall.at[band, 2 + ring],
            a1_send.at[band, k - 1], a1_recv.at[band, k - 1], ring_at(k),
        )

    def forward(band, part):
        return remote(
            xall.at[band, 4 + part], xall.at[band, part],
            fw_send.at[band, part], fw_recv.at[band, part], group_next,
        )

    def send_out(band):
        for k in (1, 2, 3):
            a1_copy(band, k).start()

    @pl.loop(0, BANDS + LAG)
    def _(i):
        @pl.when(i < BANDS)
        def _():
            for step, rim in ((1, 0), (2, 2), (3, 1), (3, 3)):
                pl.when(i == step)(lambda rim=rim: rims[rim].wait())

            conv(i)
            pl.when(has_next)(lambda: tm_copy(i).start())

        @pl.when(i >= LAG)
        def _():
            band = i - LAG
            with jax.named_scope("tm_wait"):
                pl.when(has_prev)(lambda: tm_copy(band).wait_recv())
            temporal(band)
            pl.when(band < 2)(lambda: send_out(band))
            xall[band, 2 + ring] = abuf[band, ring]
            for part in (0, 1):
                pl.when(has_group_next & (ring == part + 2))(
                    lambda part=part: forward(band, part).start()
                )

    def a2_copy(band, k):
        to = lax.rem(ring + k, RING)
        return remote(
            mb.at[band, to], mback.at[band, ring],
            a2_send.at[band, k - 1], a2_recv.at[band, k - 1], ring_at(k),
        )

    for i in (10, 11, 12, 13):
        loads[i].wait()

    @jax.named_scope("keys_values")
    def keys_values(band, start, count):
        tokens = xall[band, start : start + count].reshape(count * 128, 256)
        for buffer, weight in ((kb, wqkv[1]), (vb, wqkv[2])):
            made = dot(tokens, weight).astype(BF16)
            buffer[band, start : start + count] = made.reshape(count, 8, 16, 256)

    @jax.named_scope("attend")
    def attend(band, half):
        jobs = [(cell, half) for cell in range(8)]
        zero = jnp.zeros((64, 128), BF16)

        def doubled(buffer, cell, half):
            rows = buffer[band, 2 * half : 2 * half + 4, cell].reshape(64, 256)
            upper = jnp.concatenate([rows[:, :128], zero], axis=1)
            return jnp.concatenate([upper, jnp.concatenate([zero, rows[:, 128:]], axis=1)], axis=0)

        expos = []
        for cell, half in jobs:
            query = qb[band, 2 * half : 2 * half + 2, cell]
            spread = (query[:, None] * hmask[...][None]).reshape(128, 256)
            scores = lax.dot_general(
                doubled(kb, cell, half), spread, (((1,), (1,)), ((), ())),
                preferred_element_type=F32,
            )
            scores = scores * (1.4426950408889634 * 32**-0.5) + bias[half]
            expos.append(scores.reshape(2, 64, 128))
        expos = [jnp.exp2(e - jnp.max(e, axis=1, keepdims=True)) for e in expos]
        norms = [1.0 / jnp.sum(e, axis=1, keepdims=True) for e in expos]
        head = (iota((2, 16, 256), 2) >> 5) & 3
        for (cell, half), expo, norm in zip(jobs, expos, norms):
            weights = (expo * norm).astype(BF16).reshape(128, 128)
            mixed = lax.dot_general(
                weights, doubled(vb, cell, half), (((0,), (0,)), ((), ())),
                preferred_element_type=F32,
            ).reshape(2, 4, 16, 256)
            own = mixed[:, 0]
            for h in range(1, 4):
                own = jnp.where(head == h, mixed[:, h], own)
            mb[band, 2 * half : 2 * half + 2, 16 * cell : 16 * cell + 16] = own.astype(BF16)

    def send_back(band, half):
        for k in (1, 2, 3):
            to = lax.rem(ring + k, RING)
            pl.when(lax.div(to, 2) == half)(lambda k=k: a2_copy(band, k).start())

        @pl.when(lax.div(ring, 2) == half)
        def _():
            mback[band, ring] = mb[band, ring]

    @jax.named_scope("a1_wait")
    def arrive(band, source):
        k = lax.rem(ring + RING - source, RING)

        @pl.when(k > 0)
        def _():
            a1_copy(band, k).wait_recv()
            if source >= 2:
                pl.when(has_group_next)(lambda: forward(band, source - 2).start())

    arrive(0, 3)
    arrive(0, 2)
    send_out(2)

    @pl.loop(0, BANDS + 1)
    def _(i):
        @pl.when(i < BANDS)
        def _():
            arrive(i, 1)
            arrive(i, 0)
            with jax.named_scope("queries"):
                tokens = xall[i, 2:6].reshape(512, 256)
                qb[i] = dot(tokens, wqkv[0]).astype(BF16).reshape(4, 8, 16, 256)
            keys_values(i, 2, 4)

        @pl.when(i < BANDS - 1)
        def _():
            arrive(i + 1, 3)
            arrive(i + 1, 2)
            pl.when(i == 0)(lambda: send_out(3))

        @pl.when(i >= 1)
        def _():
            band = i - 1
            with jax.named_scope("fw_wait"):
                for part in (0, 1):
                    pl.when(has_group_prev)(lambda part=part: forward(band, part).wait_recv())
            keys_values(band, 0, 2)
            attend(band, 0)
            send_back(band, 0)

        @pl.when(i < BANDS)
        def _():
            attend(i, 1)
            send_back(i, 1)

    def store(band):
        rows, columns = (pl.ds(start, size) for start, size in zip(corner(band), (4, 8)))
        return pltpu.make_async_copy(
            res.at[rows, columns], out_hbm.at[rows, columns], store_sem.at[band]
        )

    @pl.loop(0, BANDS)
    def _(band):
        with jax.named_scope('a2_wait'):
          for k in (1, 2, 3):
            a2_copy(band, k).wait()
        y0, c0 = corner(band)
        with jax.named_scope("outproj"):
            total = dot(mback[band].reshape(512, 256), wo[...])
            total = total + hidden[band].reshape(512, 256).astype(F32)
            total = total.astype(BF16).reshape(RING, 4, 2, 16, 256)
            for q in range(RING):
                res[pl.ds(y0, 4), pl.ds(c0 + 2 * q, 2)] = total[q]
        store(band).start()

    @pl.loop(0, BANDS)
    def _(band):
        pl.when(has_next)(lambda: tm_copy(band).wait_send())
        for part in (0, 1):
            pl.when(has_group_next)(lambda part=part: forward(band, part).wait_send())
        for k in (1, 2, 3):
            a1_copy(band, k).wait_send()

        store(band).wait()


def reorder(y_hbm, out_hbm, perm, res, ov, load_sem, store_sem):
    parts = [pl.ds(2 * i, 2) for i in range(4)]
    loads = [
        pltpu.make_async_copy(y_hbm.at[rows], res.at[rows], load_sem.at[i])
        for i, rows in enumerate(parts)
    ]
    stores = [
        pltpu.make_async_copy(ov.at[:, rows], out_hbm.at[:, rows], store_sem.at[i])
        for i, rows in enumerate(parts)
    ]
    for load in loads:
        load.start()
    perm[...] = swap()
    for i in range(4):
        loads[i].wait()
        for y in (2 * i, 2 * i + 1):
            o = dot(perm[...], res[y].reshape(256, 256)).astype(BF16)
            ov[:, y] = o.reshape(16, 16, 256)
        stores[i].start()
    for store in stores:
        store.wait()


def solution(mesh):
    tm_count = mesh.shape["tm"]

    def step(x, norm_gain, conv_space, conv_time, attn_gain, wq, wk, wv, wo):
        def vmem(*shape, dtype=BF16):
            return pltpu.VMEM(shape, dtype)

        dma = pltpu.SemaphoreType.DMA
        anywhere = pl.BlockSpec(memory_space=pltpu.HBM)
        here = pl.BlockSpec(memory_space=pltpu.VMEM)
        made = pl.pallas_call(
            functools.partial(kernel, tm_count),
            out_shape=jax.ShapeDtypeStruct((8, 16, 16, 256), BF16),
            in_specs=[
                anywhere, here, anywhere, anywhere, here,
                anywhere, anywhere, anywhere, anywhere,
            ],
            out_specs=anywhere,
            scratch_shapes=[
                vmem(16, 8, 16, 256), vmem(3, 3, 256, 256), vmem(3, 256, 256),
                vmem(3, 256, 256), vmem(256, 256),
                vmem(256, 256), vmem(32, 256), vmem(512, 32), vmem(2, 128, 128, dtype=F32),
                vmem(4, 16, 256),
                vmem(10, 18, 16, 256), vmem(8, 16, 16, 256), vmem(BANDS, 512, 256),
                vmem(BANDS, 2, 32, 256), vmem(BANDS, 2, 32, 256), vmem(BANDS, 4, 128, 256),
                vmem(BANDS, 4, 128, 256), vmem(BANDS, 6, 128, 256),
                vmem(BANDS, 4, 8, 16, 256), vmem(BANDS, 6, 8, 16, 256),
                vmem(BANDS, 6, 8, 16, 256), vmem(BANDS, 4, 128, 256),
                vmem(BANDS, 4, 128, 256), vmem(8, 16, 16, 256),
                dma((14,)), dma((BANDS,)), dma((4,)), dma((4,)), dma((BANDS,)), dma((BANDS,)),
                dma((BANDS, 3)), dma((BANDS, 3)), dma((BANDS, 2)), dma((BANDS, 2)),
                dma((BANDS, 3)), dma((BANDS, 3)),
            ],
            compiler_params=pltpu.CompilerParams(
                collective_id=0, has_side_effects=True, vmem_limit_bytes=60 << 20
            ),
            name="encoder_block",
        )(
            x, norm_gain.reshape(1, -1), conv_space, conv_time, attn_gain.reshape(1, -1),
            wq, wk, wv, wo,
        )
        return pl.pallas_call(
            reorder,
            out_shape=jax.ShapeDtypeStruct(x.shape, x.dtype),
            in_specs=[anywhere],
            out_specs=anywhere,
            scratch_shapes=[
                vmem(256, 256), vmem(8, 16, 16, 256), vmem(16, 8, 16, 256), dma((4,)), dma((4,)),
            ],
            compiler_params=pltpu.CompilerParams(vmem_limit_bytes=60 << 20),
            name="reorder",
        )(made)

    tile = P("tm", "row", "col", None)
    return jax.shard_map(
        step,
        mesh=mesh,
        in_specs=(tile, P(), P(), P(), P(), P(), P(), P(), P()),
        out_specs=tile,
        check_vma=False,
    )
```

```python
import functools

import jax
import jax.numpy as jnp
from jax import lax
from jax.experimental import pallas as pl
from jax.experimental.pallas import tpu as pltpu
from jax.sharding import PartitionSpec as P

RING = 4
BANDS = 4
LAG = 2
MESH = pl.DeviceIdType.MESH
F32 = jnp.float32
BF16 = jnp.bfloat16


def dot(a, b):
    return jnp.dot(a, b, preferred_element_type=F32)


def iota(shape, dim):
    return lax.broadcasted_iota(jnp.int32, shape, dim)


def swap():
    r, s = iota((256, 256), 0), iota((256, 256), 1)
    return (((r >> 4) == (s & 15)) & ((r & 15) == (s >> 4))).astype(F32).astype(BF16)


def kernel(
    tm_count,
    x_hbm, ng_ref, cs_hbm, ct_hbm, ag_ref, wq_hbm, wk_hbm, wv_hbm, wo_hbm,
    out_hbm,
    xs, cs, ct, wqkv, wo,
    perm, pick, place, bias, hmask,
    ext, xp, sp, hsend, hrecv, hidden, abuf, xall, qb, kb, vb, mb, mback, res,
    load_sem, store_sem, rim_send, rim_recv, th_send, th_recv,
    a1_send, a1_recv, fw_send, fw_recv, a2_send, a2_recv,
):
    tm, row, col = (lax.axis_index(a) for a in ("tm", "row", "col"))
    ring, group = lax.rem(tm, RING), lax.div(tm, RING)
    groups = tm_count // RING

    def ring_at(k):
        return {"tm": group * RING + lax.rem(ring + k, RING)}

    core = {"row": 1 - row}
    side = {"col": 1 - col}
    diag = {"row": 1 - row, "col": 1 - col}
    has_prev, has_next = tm > 0, tm < tm_count - 1
    has_group_prev, has_group_next = group > 0, group < groups - 1
    tm_next, tm_prev = ({"tm": lax.rem(tm + d, tm_count)} for d in (1, tm_count - 1))
    group_next, group_prev = (
        {"tm": lax.rem(group + d, groups) * RING + ring} for d in (1, groups - 1)
    )

    row_halves = (4 * (1 - row), 4 * row)
    loads = [
        pltpu.make_async_copy(src, dst, load_sem.at[i])
        for i, (src, dst) in enumerate(
            [(x_hbm.at[:, y0 + k], xs.at[:, y0 + k]) for y0 in row_halves for k in range(4)]
            + [
                (cs_hbm, cs), (ct_hbm, ct), (wq_hbm, wqkv.at[0]),
                (wk_hbm, wqkv.at[1]), (wv_hbm, wqkv.at[2]), (wo_hbm, wo),
            ]
        )
    ]
    for load in loads[:8]:
        load.start()

    barrier = pltpu.get_barrier_semaphore()
    def greet(partner):
        pl.semaphore_signal(barrier, inc=1, device_id=partner, device_id_type=MESH)

    partners = (core, side, diag, ring_at(1), ring_at(2), ring_at(3))
    for partner in partners:
        greet(partner)
    pl.when(has_prev)(lambda: greet(tm_prev))
    pl.when(has_group_prev)(lambda: greet(group_prev))

    def remote(src, dst, send, recv, where):
        return pltpu.make_async_remote_copy(
            src_ref=src, dst_ref=dst, send_sem=send, recv_sem=recv,
            device_id=where, device_id_type=MESH,
        )

    perm[...] = swap()
    r, s = iota((32, 256), 0), iota((32, 256), 1)
    pick[...] = (s == (r & 15) * 16 + 14 + (r >> 4)).astype(F32).astype(BF16)
    r, s = iota((512, 32), 0), iota((512, 32), 1)
    lag, cell, frame = r >> 8, (r >> 4) & 15, r & 15
    hit = (s == (frame + 1 - lag) * 16 + cell) & (frame <= lag) & (tm > 0)
    place[...] = hit.astype(F32).astype(BF16)
    key, lane = iota((128, 128), 0) & 63, iota((128, 128), 1)
    query = (lane & 15) + 16 * (lane >> 6)
    for half in range(2):
        first = jnp.where(group == 0, 32 - 32 * half, 0)
        seen = (key > query) & (key <= query + 32) & (key >= first)
        bias[half] = jnp.where(seen, 0.0, -1e30).astype(F32)
    h, lane = iota((4, 16, 256), 0), iota((4, 16, 256), 2)
    hmask[...] = (h == ((lane >> 5) & 3)).astype(F32).astype(BF16)
    ext[9 * row] = jnp.zeros((18, 16, 256), BF16)
    for y in range(10):
        ext[y, 17 * col] = jnp.zeros((16, 256), BF16)

    @jax.named_scope("norm_rows")
    def norm_rows(half):
        for i in range(4):
            loads[4 * half + i].wait()
        for i in range(4):
            y = row_halves[half] + i
            v = dot(perm[...], xs[:, y].reshape(256, 256))
            scale = lax.rsqrt(jnp.mean(v * v, axis=-1, keepdims=True) + 1e-6)
            ext[y + 1, pl.ds(1, 16)] = (v * scale * ng_ref[...]).astype(BF16).reshape(16, 16, 256)
            xp[y] = v.astype(BF16).reshape(16, 16, 256)

    @pl.when(tm == 0)
    def _():
        hrecv[...] = jnp.zeros(hrecv.shape, BF16)

    @pl.when(group == 0)
    def _():
        for band in range(BANDS):
            xall[band, 0:2] = jnp.zeros((2, 128, 256), BF16)

    for load in loads[8:]:
        load.start()
    norm_rows(0)
    with jax.named_scope("barrier"):
        later = has_next.astype(jnp.int32) + has_group_next.astype(jnp.int32)
        pl.semaphore_wait(barrier, len(partners) + later)
    rim_y, rim_x = 8 - 7 * row, 16 - 15 * col
    rims = [
        remote(
            ext.at[rim_y, pl.ds(1, 16)], ext.at[9 * row, pl.ds(1, 16)],
            rim_send.at[0], rim_recv.at[0], core,
        ),
        remote(
            ext.at[rim_y, rim_x], ext.at[9 * row, 17 * col],
            rim_send.at[1], rim_recv.at[1], diag,
        ),
    ] + [
        remote(
            ext.at[pl.ds(first, rows), rim_x], ext.at[pl.ds(first, rows), 17 * col],
            rim_send.at[i], rim_recv.at[i], side,
        )
        for i, first, rows in ((2, 1 + 3 * row, 5), (3, 6 - 5 * row, 3))
    ]
    rims[0].start()
    rims[1].start()

    norm_rows(1)
    rims[2].start()
    rims[3].start()
    loads[8].wait()
    loads[9].wait()

    def corner(band):
        return 4 * ((row + band) & 1), 8 * ((col + (band >> 1)) & 1)

    @jax.named_scope("conv")
    def conv(band):
        y0, c0 = corner(band)
        total = None
        for dy in range(3):
            for dx in range(3):
                cells = ext[pl.ds(y0 + dy, 4), pl.ds(c0 + dx, 8)].reshape(512, 256)
                term = dot(cells, cs[dy, dx])
                total = term if total is None else total + term
        act = (0.5 * total * (1.0 + jnp.tanh(0.5 * total))).astype(BF16)
        sp[band] = act
        for half in range(2):
            last = dot(pick[...], act[256 * half : 256 * half + 256])
            hsend[band, half] = last.astype(BF16)

    def tm_copy(band):
        return remote(
            hsend.at[band], hrecv.at[band], th_send.at[band], th_recv.at[band], tm_next
        )

    def shares(buffer, band, tokens):
        tokens = tokens.reshape(4, 8, 16, 256)
        for q in range(RING):
            buffer[band, q] = tokens[:, 2 * q : 2 * q + 2].reshape(128, 256)

    @jax.named_scope("temporal")
    def temporal(band):
        act = sp[band]
        wide = act.astype(F32).reshape(32, 16, 256)
        early = [dot(place[...], hrecv[band, half]) for half in range(2)]
        frame = iota((32, 16, 256), 1)
        total = dot(act, ct[0])
        for lag in (1, 2):
            before = [e[256 * (lag - 1) : 256 * lag] for e in early]
            before = jnp.concatenate(before, axis=0).reshape(32, 16, 256)
            moved = jnp.where(frame < lag, before, pltpu.roll(wide, lag, 1))
            total = total + dot(moved.astype(BF16).reshape(512, 256), ct[lag])
        y0, c0 = corner(band)
        own = xp[pl.ds(y0, 4), pl.ds(c0, 8)].reshape(512, 256).astype(F32)
        hid = (own + total).astype(BF16)
        shares(hidden, band, hid)
        v = hid.astype(F32)
        scale = lax.rsqrt(jnp.mean(v * v, axis=-1, keepdims=True) + 1e-6)
        shares(abuf, band, (v * scale * ag_ref[...]).astype(BF16))

    def a1_copy(band, k):
        to = lax.rem(ring + k, RING)
        return remote(
            abuf.at[band, to], xall.at[band, 2 + ring],
            a1_send.at[band, k - 1], a1_recv.at[band, k - 1], ring_at(k),
        )

    def forward(band, part):
        return remote(
            xall.at[band, 4 + part], xall.at[band, part],
            fw_send.at[band, part], fw_recv.at[band, part], group_next,
        )

    def send_out(band):
        for k in (2, 1, 3):
            a1_copy(band, k).start()

    @pl.loop(0, BANDS + LAG)
    def _(i):
        @pl.when(i < BANDS)
        def _():
            for step, rim in ((1, 0), (2, 2), (3, 1), (3, 3)):
                pl.when(i == step)(lambda rim=rim: rims[rim].wait())

            conv(i)
            pl.when(has_next)(lambda: tm_copy(i).start())

        @pl.when(i >= LAG)
        def _():
            band = i - LAG
            with jax.named_scope("tm_wait"):
                pl.when(has_prev)(lambda: tm_copy(band).wait_recv())
            temporal(band)
            pl.when(band < 2)(lambda: send_out(band))
            xall[band, 2 + ring] = abuf[band, ring]
            for part in (0, 1):
                pl.when(has_group_next & (ring == part + 2))(
                    lambda part=part: forward(band, part).start()
                )

    def a2_copy(band, k):
        to = lax.rem(ring + k, RING)
        return remote(
            mb.at[band, to], mback.at[band, ring],
            a2_send.at[band, k - 1], a2_recv.at[band, k - 1], ring_at(k),
        )

    for i in (10, 11, 12, 13):
        loads[i].wait()

    @jax.named_scope("keys_values")
    def keys_values(band, start, count):
        tokens = xall[band, start : start + count].reshape(count * 128, 256)
        for buffer, weight in ((kb, wqkv[1]), (vb, wqkv[2])):
            made = dot(tokens, weight).astype(BF16)
            buffer[band, start : start + count] = made.reshape(count, 8, 16, 256)

    @jax.named_scope("attend")
    def attend(band, half):
        jobs = [(cell, half) for cell in range(8)]
        zero = jnp.zeros((64, 128), BF16)

        def doubled(buffer, cell, half):
            rows = buffer[band, 2 * half : 2 * half + 4, cell].reshape(64, 256)
            upper = jnp.concatenate([rows[:, :128], zero], axis=1)
            return jnp.concatenate([upper, jnp.concatenate([zero, rows[:, 128:]], axis=1)], axis=0)

        expos = []
        for cell, half in jobs:
            query = qb[band, 2 * half : 2 * half + 2, cell]
            spread = (query[:, None] * hmask[...][None]).reshape(128, 256)
            scores = lax.dot_general(
                doubled(kb, cell, half), spread, (((1,), (1,)), ((), ())),
                preferred_element_type=F32,
            )
            scores = scores * (1.4426950408889634 * 32**-0.5) + bias[half]
            expos.append(scores.reshape(2, 64, 128))
        expos = [jnp.exp2(e - jnp.max(e, axis=1, keepdims=True)) for e in expos]
        norms = [1.0 / jnp.sum(e, axis=1, keepdims=True) for e in expos]
        head = (iota((2, 16, 256), 2) >> 5) & 3
        for (cell, half), expo, norm in zip(jobs, expos, norms):
            weights = (expo * norm).astype(BF16).reshape(128, 128)
            mixed = lax.dot_general(
                weights, doubled(vb, cell, half), (((0,), (0,)), ((), ())),
                preferred_element_type=F32,
            ).reshape(2, 4, 16, 256)
            own = mixed[:, 0]
            for h in range(1, 4):
                own = jnp.where(head == h, mixed[:, h], own)
            mb[band, 2 * half : 2 * half + 2, 16 * cell : 16 * cell + 16] = own.astype(BF16)

    def send_back(band, half):
        for k in (1, 2, 3):
            to = lax.rem(ring + k, RING)
            pl.when(lax.div(to, 2) == half)(lambda k=k: a2_copy(band, k).start())

        @pl.when(lax.div(ring, 2) == half)
        def _():
            mback[band, ring] = mb[band, ring]

    @jax.named_scope("a1_wait")
    def arrive(band, source):
        k = lax.rem(ring + RING - source, RING)

        @pl.when(k > 0)
        def _():
            a1_copy(band, k).wait_recv()
            if source >= 2:
                pl.when(has_group_next)(lambda: forward(band, source - 2).start())

    arrive(0, 3)
    arrive(0, 2)
    send_out(2)

    @pl.loop(0, BANDS + 1)
    def _(i):
        @pl.when(i < BANDS)
        def _():
            arrive(i, 1)
            arrive(i, 0)
            with jax.named_scope("queries"):
                tokens = xall[i, 2:6].reshape(512, 256)
                qb[i] = dot(tokens, wqkv[0]).astype(BF16).reshape(4, 8, 16, 256)
            keys_values(i, 2, 4)

        @pl.when(i < BANDS - 1)
        def _():
            arrive(i + 1, 3)
            arrive(i + 1, 2)
            pl.when(i == 0)(lambda: send_out(3))

        @pl.when(i >= 1)
        def _():
            band = i - 1
            with jax.named_scope("fw_wait"):
                for part in (0, 1):
                    pl.when(has_group_prev)(lambda part=part: forward(band, part).wait_recv())
            keys_values(band, 0, 2)
            attend(band, 0)
            send_back(band, 0)

        @pl.when(i < BANDS)
        def _():
            attend(i, 1)
            send_back(i, 1)

    def store(band):
        rows, columns = (pl.ds(start, size) for start, size in zip(corner(band), (4, 8)))
        return pltpu.make_async_copy(
            res.at[rows, columns], out_hbm.at[rows, columns], store_sem.at[band]
        )

    @pl.loop(0, BANDS)
    def _(band):
        with jax.named_scope('a2_wait'):
          for k in (1, 2, 3):
            a2_copy(band, k).wait()
        y0, c0 = corner(band)
        with jax.named_scope("outproj"):
            total = dot(mback[band].reshape(512, 256), wo[...])
            total = total + hidden[band].reshape(512, 256).astype(F32)
            total = total.astype(BF16).reshape(RING, 4, 2, 16, 256)
            for q in range(RING):
                res[pl.ds(y0, 4), pl.ds(c0 + 2 * q, 2)] = total[q]
        store(band).start()

    @pl.loop(0, BANDS)
    def _(band):
        pl.when(has_next)(lambda: tm_copy(band).wait_send())
        for part in (0, 1):
            pl.when(has_group_next)(lambda part=part: forward(band, part).wait_send())
        for k in (1, 2, 3):
            a1_copy(band, k).wait_send()

        store(band).wait()


def reorder(y_hbm, out_hbm, perm, res, ov, load_sem, store_sem):
    parts = [pl.ds(2 * i, 2) for i in range(4)]
    loads = [
        pltpu.make_async_copy(y_hbm.at[rows], res.at[rows], load_sem.at[i])
        for i, rows in enumerate(parts)
    ]
    stores = [
        pltpu.make_async_copy(ov.at[:, rows], out_hbm.at[:, rows], store_sem.at[i])
        for i, rows in enumerate(parts)
    ]
    for load in loads[:8]:
        load.start()
    perm[...] = swap()
    for i in range(4):
        loads[i].wait()
        for y in (2 * i, 2 * i + 1):
            o = dot(perm[...], res[y].reshape(256, 256)).astype(BF16)
            ov[:, y] = o.reshape(16, 16, 256)
        stores[i].start()
    for store in stores:
        store.wait()


def solution(mesh):
    tm_count = mesh.shape["tm"]

    def step(x, norm_gain, conv_space, conv_time, attn_gain, wq, wk, wv, wo):
        def vmem(*shape, dtype=BF16):
            return pltpu.VMEM(shape, dtype)

        dma = pltpu.SemaphoreType.DMA
        anywhere = pl.BlockSpec(memory_space=pltpu.HBM)
        here = pl.BlockSpec(memory_space=pltpu.VMEM)
        made = pl.pallas_call(
            functools.partial(kernel, tm_count),
            out_shape=jax.ShapeDtypeStruct((8, 16, 16, 256), BF16),
            in_specs=[
                anywhere, here, anywhere, anywhere, here,
                anywhere, anywhere, anywhere, anywhere,
            ],
            out_specs=anywhere,
            scratch_shapes=[
                vmem(16, 8, 16, 256), vmem(3, 3, 256, 256), vmem(3, 256, 256),
                vmem(3, 256, 256), vmem(256, 256),
                vmem(256, 256), vmem(32, 256), vmem(512, 32), vmem(2, 128, 128, dtype=F32),
                vmem(4, 16, 256),
                vmem(10, 18, 16, 256), vmem(8, 16, 16, 256), vmem(BANDS, 512, 256),
                vmem(BANDS, 2, 32, 256), vmem(BANDS, 2, 32, 256), vmem(BANDS, 4, 128, 256),
                vmem(BANDS, 4, 128, 256), vmem(BANDS, 6, 128, 256),
                vmem(BANDS, 4, 8, 16, 256), vmem(BANDS, 6, 8, 16, 256),
                vmem(BANDS, 6, 8, 16, 256), vmem(BANDS, 4, 128, 256),
                vmem(BANDS, 4, 128, 256), vmem(8, 16, 16, 256),
                dma((14,)), dma((BANDS,)), dma((4,)), dma((4,)), dma((BANDS,)), dma((BANDS,)),
                dma((BANDS, 3)), dma((BANDS, 3)), dma((BANDS, 2)), dma((BANDS, 2)),
                dma((BANDS, 3)), dma((BANDS, 3)),
            ],
            compiler_params=pltpu.CompilerParams(
                collective_id=0, has_side_effects=True, vmem_limit_bytes=60 << 20
            ),
            name="encoder_block",
        )(
            x, norm_gain.reshape(1, -1), conv_space, conv_time, attn_gain.reshape(1, -1),
            wq, wk, wv, wo,
        )
        return pl.pallas_call(
            reorder,
            out_shape=jax.ShapeDtypeStruct(x.shape, x.dtype),
            in_specs=[anywhere],
            out_specs=anywhere,
            scratch_shapes=[
                vmem(256, 256), vmem(8, 16, 16, 256), vmem(16, 8, 16, 256), dma((4,)), dma((4,)),
            ],
            compiler_params=pltpu.CompilerParams(vmem_limit_bytes=60 << 20),
            name="reorder",
        )(made)

    tile = P("tm", "row", "col", None)
    return jax.shard_map(
        step,
        mesh=mesh,
        in_specs=(tile, P(), P(), P(), P(), P(), P(), P(), P()),
        out_specs=tile,
        check_vma=False,
    )
```

```python
import functools

import jax
import jax.numpy as jnp
from jax import lax
from jax.experimental import pallas as pl
from jax.experimental.pallas import tpu as pltpu
from jax.sharding import PartitionSpec as P

RING = 4
BANDS = 4
LAG = 2
MESH = pl.DeviceIdType.MESH
F32 = jnp.float32
BF16 = jnp.bfloat16


def dot(a, b):
    return jnp.dot(a, b, preferred_element_type=F32)


def iota(shape, dim):
    return lax.broadcasted_iota(jnp.int32, shape, dim)


def swap():
    r, s = iota((256, 256), 0), iota((256, 256), 1)
    return (((r >> 4) == (s & 15)) & ((r & 15) == (s >> 4))).astype(F32).astype(BF16)


def kernel(
    tm_count,
    x_hbm, ng_ref, cs_hbm, ct_hbm, ag_ref, wq_hbm, wk_hbm, wv_hbm, wo_hbm,
    out_hbm,
    xs, cs, ct, wqkv, wo,
    perm, pick, place, bias, hmask,
    ext, xp, sp, hsend, hrecv, hidden, abuf, xall, qb, kb, vb, mb, mback, res,
    load_sem, store_sem, rim_send, rim_recv, th_send, th_recv,
    a1_send, a1_recv, fw_send, fw_recv, a2_send, a2_recv,
):
    tm, row, col = (lax.axis_index(a) for a in ("tm", "row", "col"))
    ring, group = lax.rem(tm, RING), lax.div(tm, RING)
    groups = tm_count // RING

    def ring_at(k):
        return {"tm": group * RING + lax.rem(ring + k, RING)}

    core = {"row": 1 - row}
    side = {"col": 1 - col}
    diag = {"row": 1 - row, "col": 1 - col}
    has_prev, has_next = tm > 0, tm < tm_count - 1
    has_group_prev, has_group_next = group > 0, group < groups - 1
    tm_next, tm_prev = ({"tm": lax.rem(tm + d, tm_count)} for d in (1, tm_count - 1))
    group_next, group_prev = (
        {"tm": lax.rem(group + d, groups) * RING + ring} for d in (1, groups - 1)
    )

    row_halves = (4 * (1 - row), 4 * row)
    loads = [
        pltpu.make_async_copy(src, dst, load_sem.at[i])
        for i, (src, dst) in enumerate(
            [(x_hbm.at[:, y0 + k], xs.at[:, y0 + k]) for y0 in row_halves for k in range(4)]
            + [
                (cs_hbm, cs), (ct_hbm, ct), (wq_hbm, wqkv.at[0]),
                (wk_hbm, wqkv.at[1]), (wv_hbm, wqkv.at[2]), (wo_hbm, wo),
            ]
        )
    ]
    for load in loads:
        load.start()

    barrier = pltpu.get_barrier_semaphore()
    def greet(partner):
        pl.semaphore_signal(barrier, inc=1, device_id=partner, device_id_type=MESH)

    partners = (core, side, diag, ring_at(1), ring_at(2), ring_at(3))
    for partner in partners:
        greet(partner)
    pl.when(has_prev)(lambda: greet(tm_prev))
    pl.when(has_group_prev)(lambda: greet(group_prev))

    def remote(src, dst, send, recv, where):
        return pltpu.make_async_remote_copy(
            src_ref=src, dst_ref=dst, send_sem=send, recv_sem=recv,
            device_id=where, device_id_type=MESH,
        )

    perm[...] = swap()
    r, s = iota((32, 256), 0), iota((32, 256), 1)
    pick[...] = (s == (r & 15) * 16 + 14 + (r >> 4)).astype(F32).astype(BF16)
    r, s = iota((512, 32), 0), iota((512, 32), 1)
    lag, cell, frame = r >> 8, (r >> 4) & 15, r & 15
    hit = (s == (frame + 1 - lag) * 16 + cell) & (frame <= lag) & (tm > 0)
    place[...] = hit.astype(F32).astype(BF16)
    key, lane = iota((128, 128), 0) & 63, iota((128, 128), 1)
    query = (lane & 15) + 16 * (lane >> 6)
    for half in range(2):
        first = jnp.where(group == 0, 32 - 32 * half, 0)
        seen = (key > query) & (key <= query + 32) & (key >= first)
        bias[half] = jnp.where(seen, 0.0, -1e30).astype(F32)
    h, lane = iota((4, 16, 256), 0), iota((4, 16, 256), 2)
    hmask[...] = (h == ((lane >> 5) & 3)).astype(F32).astype(BF16)
    ext[9 * row] = jnp.zeros((18, 16, 256), BF16)
    for y in range(10):
        ext[y, 17 * col] = jnp.zeros((16, 256), BF16)

    @jax.named_scope("norm_rows")
    def norm_rows(half):
        for i in range(4):
            loads[4 * half + i].wait()
        for i in range(4):
            y = row_halves[half] + i
            v = dot(perm[...], xs[:, y].reshape(256, 256))
            scale = lax.rsqrt(jnp.mean(v * v, axis=-1, keepdims=True) + 1e-6)
            ext[y + 1, pl.ds(1, 16)] = (v * scale * ng_ref[...]).astype(BF16).reshape(16, 16, 256)
            xp[y] = v.astype(BF16).reshape(16, 16, 256)

    @pl.when(tm == 0)
    def _():
        hrecv[...] = jnp.zeros(hrecv.shape, BF16)

    @pl.when(group == 0)
    def _():
        for band in range(BANDS):
            xall[band, 0:2] = jnp.zeros((2, 128, 256), BF16)

    norm_rows(0)
    norm_rows(1)
    with jax.named_scope("barrier"):
        later = has_next.astype(jnp.int32) + has_group_next.astype(jnp.int32)
        pl.semaphore_wait(barrier, len(partners) + later)
    rim_y, rim_x = 8 - 7 * row, 16 - 15 * col
    rims = [
        remote(
            ext.at[rim_y, pl.ds(1, 16)], ext.at[9 * row, pl.ds(1, 16)],
            rim_send.at[0], rim_recv.at[0], core,
        ),
        remote(
            ext.at[rim_y, rim_x], ext.at[9 * row, 17 * col],
            rim_send.at[1], rim_recv.at[1], diag,
        ),
    ] + [
        remote(
            ext.at[pl.ds(first, rows), rim_x], ext.at[pl.ds(first, rows), 17 * col],
            rim_send.at[i], rim_recv.at[i], side,
        )
        for i, first, rows in ((2, 1 + 3 * row, 5), (3, 6 - 5 * row, 3))
    ]
    rims[0].start()
    rims[1].start()

    rims[2].start()
    rims[3].start()
    loads[8].wait()
    loads[9].wait()

    def corner(band):
        return 4 * ((row + band) & 1), 8 * ((col + (band >> 1)) & 1)

    @jax.named_scope("conv")
    def conv(band):
        y0, c0 = corner(band)
        total = None
        for dy in range(3):
            for dx in range(3):
                cells = ext[pl.ds(y0 + dy, 4), pl.ds(c0 + dx, 8)].reshape(512, 256)
                term = dot(cells, cs[dy, dx])
                total = term if total is None else total + term
        act = (0.5 * total * (1.0 + jnp.tanh(0.5 * total))).astype(BF16)
        sp[band] = act
        for half in range(2):
            last = dot(pick[...], act[256 * half : 256 * half + 256])
            hsend[band, half] = last.astype(BF16)

    def tm_copy(band):
        return remote(
            hsend.at[band], hrecv.at[band], th_send.at[band], th_recv.at[band], tm_next
        )

    def shares(buffer, band, tokens):
        tokens = tokens.reshape(4, 8, 16, 256)
        for q in range(RING):
            buffer[band, q] = tokens[:, 2 * q : 2 * q + 2].reshape(128, 256)

    @jax.named_scope("temporal")
    def temporal(band):
        act = sp[band]
        wide = act.astype(F32).reshape(32, 16, 256)
        early = [dot(place[...], hrecv[band, half]) for half in range(2)]
        frame = iota((32, 16, 256), 1)
        total = dot(act, ct[0])
        for lag in (1, 2):
            before = [e[256 * (lag - 1) : 256 * lag] for e in early]
            before = jnp.concatenate(before, axis=0).reshape(32, 16, 256)
            moved = jnp.where(frame < lag, before, pltpu.roll(wide, lag, 1))
            total = total + dot(moved.astype(BF16).reshape(512, 256), ct[lag])
        y0, c0 = corner(band)
        own = xp[pl.ds(y0, 4), pl.ds(c0, 8)].reshape(512, 256).astype(F32)
        hid = (own + total).astype(BF16)
        shares(hidden, band, hid)
        v = hid.astype(F32)
        scale = lax.rsqrt(jnp.mean(v * v, axis=-1, keepdims=True) + 1e-6)
        shares(abuf, band, (v * scale * ag_ref[...]).astype(BF16))

    def a1_copy(band, k):
        to = lax.rem(ring + k, RING)
        return remote(
            abuf.at[band, to], xall.at[band, 2 + ring],
            a1_send.at[band, k - 1], a1_recv.at[band, k - 1], ring_at(k),
        )

    def forward(band, part):
        return remote(
            xall.at[band, 4 + part], xall.at[band, part],
            fw_send.at[band, part], fw_recv.at[band, part], group_next,
        )

    def send_out(band):
        for k in (1, 2, 3):
            a1_copy(band, k).start()

    @pl.loop(0, BANDS + LAG)
    def _(i):
        @pl.when(i < BANDS)
        def _():
            for step, rim in ((1, 0), (2, 2), (3, 1), (3, 3)):
                pl.when(i == step)(lambda rim=rim: rims[rim].wait())

            conv(i)
            pl.when(has_next)(lambda: tm_copy(i).start())

        @pl.when(i >= LAG)
        def _():
            band = i - LAG
            with jax.named_scope("tm_wait"):
                pl.when(has_prev)(lambda: tm_copy(band).wait_recv())
            temporal(band)
            pl.when(band < 2)(lambda: send_out(band))
            xall[band, 2 + ring] = abuf[band, ring]
            for part in (0, 1):
                pl.when(has_group_next & (ring == part + 2))(
                    lambda part=part: forward(band, part).start()
                )

    def a2_copy(band, k):
        to = lax.rem(ring + k, RING)
        return remote(
            mb.at[band, to], mback.at[band, ring],
            a2_send.at[band, k - 1], a2_recv.at[band, k - 1], ring_at(k),
        )

    for i in (10, 11, 12, 13):
        loads[i].wait()

    @jax.named_scope("keys_values")
    def keys_values(band, start, count):
        tokens = xall[band, start : start + count].reshape(count * 128, 256)
        for buffer, weight in ((kb, wqkv[1]), (vb, wqkv[2])):
            made = dot(tokens, weight).astype(BF16)
            buffer[band, start : start + count] = made.reshape(count, 8, 16, 256)

    @jax.named_scope("attend")
    def attend(band, half):
        jobs = [(cell, half) for cell in range(8)]
        zero = jnp.zeros((64, 128), BF16)

        def doubled(buffer, cell, half):
            rows = buffer[band, 2 * half : 2 * half + 4, cell].reshape(64, 256)
            upper = jnp.concatenate([rows[:, :128], zero], axis=1)
            return jnp.concatenate([upper, jnp.concatenate([zero, rows[:, 128:]], axis=1)], axis=0)

        expos = []
        for cell, half in jobs:
            query = qb[band, 2 * half : 2 * half + 2, cell]
            spread = (query[:, None] * hmask[...][None]).reshape(128, 256)
            scores = lax.dot_general(
                doubled(kb, cell, half), spread, (((1,), (1,)), ((), ())),
                preferred_element_type=F32,
            )
            scores = scores * (1.4426950408889634 * 32**-0.5) + bias[half]
            expos.append(scores.reshape(2, 64, 128))
        expos = [jnp.exp2(e - jnp.max(e, axis=1, keepdims=True)) for e in expos]
        norms = [1.0 / jnp.sum(e, axis=1, keepdims=True) for e in expos]
        head = (iota((2, 16, 256), 2) >> 5) & 3
        for (cell, half), expo, norm in zip(jobs, expos, norms):
            weights = (expo * norm).astype(BF16).reshape(128, 128)
            mixed = lax.dot_general(
                weights, doubled(vb, cell, half), (((0,), (0,)), ((), ())),
                preferred_element_type=F32,
            ).reshape(2, 4, 16, 256)
            own = mixed[:, 0]
            for h in range(1, 4):
                own = jnp.where(head == h, mixed[:, h], own)
            mb[band, 2 * half : 2 * half + 2, 16 * cell : 16 * cell + 16] = own.astype(BF16)

    def send_back(band, half):
        for k in (1, 2, 3):
            to = lax.rem(ring + k, RING)
            pl.when(lax.div(to, 2) == half)(lambda k=k: a2_copy(band, k).start())

        @pl.when(lax.div(ring, 2) == half)
        def _():
            mback[band, ring] = mb[band, ring]

    @jax.named_scope("a1_wait")
    def arrive(band, source):
        k = lax.rem(ring + RING - source, RING)

        @pl.when(k > 0)
        def _():
            a1_copy(band, k).wait_recv()
            if source >= 2:
                pl.when(has_group_next)(lambda: forward(band, source - 2).start())

    arrive(0, 3)
    arrive(0, 2)
    send_out(2)

    @pl.loop(0, BANDS + 1)
    def _(i):
        @pl.when(i < BANDS)
        def _():
            arrive(i, 1)
            arrive(i, 0)
            with jax.named_scope("queries"):
                tokens = xall[i, 2:6].reshape(512, 256)
                qb[i] = dot(tokens, wqkv[0]).astype(BF16).reshape(4, 8, 16, 256)
            keys_values(i, 2, 4)

        @pl.when(i < BANDS - 1)
        def _():
            arrive(i + 1, 3)
            arrive(i + 1, 2)
            pl.when(i == 0)(lambda: send_out(3))

        @pl.when(i >= 1)
        def _():
            band = i - 1
            with jax.named_scope("fw_wait"):
                for part in (0, 1):
                    pl.when(has_group_prev)(lambda part=part: forward(band, part).wait_recv())
            keys_values(band, 0, 2)
            attend(band, 0)
            send_back(band, 0)

        @pl.when(i < BANDS)
        def _():
            attend(i, 1)
            send_back(i, 1)

    def store(band):
        rows, columns = (pl.ds(start, size) for start, size in zip(corner(band), (4, 8)))
        return pltpu.make_async_copy(
            res.at[rows, columns], out_hbm.at[rows, columns], store_sem.at[band]
        )

    @pl.loop(0, BANDS)
    def _(band):
        with jax.named_scope('a2_wait'):
          for k in (1, 2, 3):
            a2_copy(band, k).wait()
        y0, c0 = corner(band)
        with jax.named_scope("outproj"):
            total = dot(mback[band].reshape(512, 256), wo[...])
            total = total + hidden[band].reshape(512, 256).astype(F32)
            total = total.astype(BF16).reshape(RING, 4, 2, 16, 256)
            for q in range(RING):
                res[pl.ds(y0, 4), pl.ds(c0 + 2 * q, 2)] = total[q]
        store(band).start()

    @pl.loop(0, BANDS)
    def _(band):
        pl.when(has_next)(lambda: tm_copy(band).wait_send())
        for part in (0, 1):
            pl.when(has_group_next)(lambda part=part: forward(band, part).wait_send())
        for k in (1, 2, 3):
            a1_copy(band, k).wait_send()

        store(band).wait()


def reorder(y_hbm, out_hbm, perm, res, ov, load_sem, store_sem):
    parts = [pl.ds(2 * i, 2) for i in range(4)]
    loads = [
        pltpu.make_async_copy(y_hbm.at[rows], res.at[rows], load_sem.at[i])
        for i, rows in enumerate(parts)
    ]
    stores = [
        pltpu.make_async_copy(ov.at[:, rows], out_hbm.at[:, rows], store_sem.at[i])
        for i, rows in enumerate(parts)
    ]
    for load in loads:
        load.start()
    perm[...] = swap()
    for i in range(4):
        loads[i].wait()
        for y in (2 * i, 2 * i + 1):
            o = dot(perm[...], res[y].reshape(256, 256)).astype(BF16)
            ov[:, y] = o.reshape(16, 16, 256)
        stores[i].start()
    for store in stores:
        store.wait()


def solution(mesh):
    tm_count = mesh.shape["tm"]

    def step(x, norm_gain, conv_space, conv_time, attn_gain, wq, wk, wv, wo):
        def vmem(*shape, dtype=BF16):
            return pltpu.VMEM(shape, dtype)

        dma = pltpu.SemaphoreType.DMA
        anywhere = pl.BlockSpec(memory_space=pltpu.HBM)
        here = pl.BlockSpec(memory_space=pltpu.VMEM)
        made = pl.pallas_call(
            functools.partial(kernel, tm_count),
            out_shape=jax.ShapeDtypeStruct((8, 16, 16, 256), BF16),
            in_specs=[
                anywhere, here, anywhere, anywhere, here,
                anywhere, anywhere, anywhere, anywhere,
            ],
            out_specs=anywhere,
            scratch_shapes=[
                vmem(16, 8, 16, 256), vmem(3, 3, 256, 256), vmem(3, 256, 256),
                vmem(3, 256, 256), vmem(256, 256),
                vmem(256, 256), vmem(32, 256), vmem(512, 32), vmem(2, 128, 128, dtype=F32),
                vmem(4, 16, 256),
                vmem(10, 18, 16, 256), vmem(8, 16, 16, 256), vmem(BANDS, 512, 256),
                vmem(BANDS, 2, 32, 256), vmem(BANDS, 2, 32, 256), vmem(BANDS, 4, 128, 256),
                vmem(BANDS, 4, 128, 256), vmem(BANDS, 6, 128, 256),
                vmem(BANDS, 4, 8, 16, 256), vmem(BANDS, 6, 8, 16, 256),
                vmem(BANDS, 6, 8, 16, 256), vmem(BANDS, 4, 128, 256),
                vmem(BANDS, 4, 128, 256), vmem(8, 16, 16, 256),
                dma((14,)), dma((BANDS,)), dma((4,)), dma((4,)), dma((BANDS,)), dma((BANDS,)),
                dma((BANDS, 3)), dma((BANDS, 3)), dma((BANDS, 2)), dma((BANDS, 2)),
                dma((BANDS, 3)), dma((BANDS, 3)),
            ],
            compiler_params=pltpu.CompilerParams(
                collective_id=0, has_side_effects=True, vmem_limit_bytes=60 << 20
            ),
            name="encoder_block",
        )(
            x, norm_gain.reshape(1, -1), conv_space, conv_time, attn_gain.reshape(1, -1),
            wq, wk, wv, wo,
        )
        return pl.pallas_call(
            reorder,
            out_shape=jax.ShapeDtypeStruct(x.shape, x.dtype),
            in_specs=[anywhere],
            out_specs=anywhere,
            scratch_shapes=[
                vmem(256, 256), vmem(8, 16, 16, 256), vmem(16, 8, 16, 256), dma((4,)), dma((4,)),
            ],
            compiler_params=pltpu.CompilerParams(vmem_limit_bytes=60 << 20),
            name="reorder",
        )(made)

    tile = P("tm", "row", "col", None)
    return jax.shard_map(
        step,
        mesh=mesh,
        in_specs=(tile, P(), P(), P(), P(), P(), P(), P(), P()),
        out_specs=tile,
        check_vma=False,
    )
```

```python
import functools

import jax
import jax.numpy as jnp
from jax import lax
from jax.experimental import pallas as pl
from jax.experimental.pallas import tpu as pltpu
from jax.sharding import PartitionSpec as P

RING = 4
BANDS = 4
LAG = 2
MESH = pl.DeviceIdType.MESH
F32 = jnp.float32
BF16 = jnp.bfloat16


def dot(a, b):
    return jnp.dot(a, b, preferred_element_type=F32)


def iota(shape, dim):
    return lax.broadcasted_iota(jnp.int32, shape, dim)


def swap():
    r, s = iota((256, 256), 0), iota((256, 256), 1)
    return (((r >> 4) == (s & 15)) & ((r & 15) == (s >> 4))).astype(F32).astype(BF16)


def kernel(
    tm_count,
    x_hbm, ng_ref, cs_hbm, ct_hbm, ag_ref, wq_hbm, wk_hbm, wv_hbm, wo_hbm,
    out_hbm,
    xs, cs, ct, wqkv, wo,
    perm, pick, place, bias, hmask,
    ext, xp, sp, hsend, hrecv, hidden, abuf, xall, qb, kb, vb, mb, mback, res,
    load_sem, store_sem, rim_send, rim_recv, th_send, th_recv,
    a1_send, a1_recv, fw_send, fw_recv, a2_send, a2_recv,
):
    tm, row, col = (lax.axis_index(a) for a in ("tm", "row", "col"))
    ring, group = lax.rem(tm, RING), lax.div(tm, RING)
    groups = tm_count // RING

    def ring_at(k):
        return {"tm": group * RING + lax.rem(ring + k, RING)}

    core = {"row": 1 - row}
    side = {"col": 1 - col}
    diag = {"row": 1 - row, "col": 1 - col}
    has_prev, has_next = tm > 0, tm < tm_count - 1
    has_group_prev, has_group_next = group > 0, group < groups - 1
    tm_next, tm_prev = ({"tm": lax.rem(tm + d, tm_count)} for d in (1, tm_count - 1))
    group_next, group_prev = (
        {"tm": lax.rem(group + d, groups) * RING + ring} for d in (1, groups - 1)
    )

    row_halves = (4 * (1 - row), 4 * row)
    loads = [
        pltpu.make_async_copy(src, dst, load_sem.at[i])
        for i, (src, dst) in enumerate(
            [(x_hbm.at[:, y0 + k], xs.at[:, y0 + k]) for y0 in row_halves for k in range(4)]
            + [
                (cs_hbm, cs), (ct_hbm, ct), (wq_hbm, wqkv.at[0]),
                (wk_hbm, wqkv.at[1]), (wv_hbm, wqkv.at[2]), (wo_hbm, wo),
            ]
        )
    ]
    for load in loads:
        load.start()

    barrier = pltpu.get_barrier_semaphore()
    def greet(partner):
        pl.semaphore_signal(barrier, inc=1, device_id=partner, device_id_type=MESH)

    partners = (core, side, diag, ring_at(1), ring_at(2), ring_at(3))
    for partner in partners:
        greet(partner)
    pl.when(has_prev)(lambda: greet(tm_prev))
    pl.when(has_group_prev)(lambda: greet(group_prev))

    def remote(src, dst, send, recv, where):
        return pltpu.make_async_remote_copy(
            src_ref=src, dst_ref=dst, send_sem=send, recv_sem=recv,
            device_id=where, device_id_type=MESH,
        )

    perm[...] = swap()
    r, s = iota((32, 256), 0), iota((32, 256), 1)
    pick[...] = (s == (r & 15) * 16 + 14 + (r >> 4)).astype(F32).astype(BF16)
    r, s = iota((512, 32), 0), iota((512, 32), 1)
    lag, cell, frame = r >> 8, (r >> 4) & 15, r & 15
    hit = (s == (frame + 1 - lag) * 16 + cell) & (frame <= lag) & (tm > 0)
    place[...] = hit.astype(F32).astype(BF16)
    key, lane = iota((128, 128), 0) & 63, iota((128, 128), 1)
    query = (lane & 15) + 16 * (lane >> 6)
    for half in range(2):
        first = jnp.where(group == 0, 32 - 32 * half, 0)
        seen = (key > query) & (key <= query + 32) & (key >= first)
        bias[half] = jnp.where(seen, 0.0, -1e30).astype(F32)
    h, lane = iota((4, 16, 256), 0), iota((4, 16, 256), 2)
    hmask[...] = (h == ((lane >> 5) & 3)).astype(F32).astype(BF16)
    ext[9 * row] = jnp.zeros((18, 16, 256), BF16)
    for y in range(10):
        ext[y, 17 * col] = jnp.zeros((16, 256), BF16)

    @jax.named_scope("norm_rows")
    def norm_rows(half):
        for i in range(4):
            loads[4 * half + i].wait()
        for i in range(4):
            y = row_halves[half] + i
            v = dot(perm[...], xs[:, y].reshape(256, 256))
            scale = lax.rsqrt(jnp.mean(v * v, axis=-1, keepdims=True) + 1e-6)
            ext[y + 1, pl.ds(1, 16)] = (v * scale * ng_ref[...]).astype(BF16).reshape(16, 16, 256)
            xp[y] = v.astype(BF16).reshape(16, 16, 256)

    @pl.when(tm == 0)
    def _():
        hrecv[...] = jnp.zeros(hrecv.shape, BF16)

    @pl.when(group == 0)
    def _():
        for band in range(BANDS):
            xall[band, 0:2] = jnp.zeros((2, 128, 256), BF16)

    norm_rows(0)
    norm_rows(1)
    with jax.named_scope("barrier"):
        later = has_next.astype(jnp.int32) + has_group_next.astype(jnp.int32)
        pl.semaphore_wait(barrier, len(partners) + later)
    rim_y, rim_x = 8 - 7 * row, 16 - 15 * col
    rims = [
        remote(
            ext.at[rim_y, pl.ds(1, 16)], ext.at[9 * row, pl.ds(1, 16)],
            rim_send.at[0], rim_recv.at[0], core,
        ),
        remote(
            ext.at[rim_y, rim_x], ext.at[9 * row, 17 * col],
            rim_send.at[1], rim_recv.at[1], diag,
        ),
    ] + [
        remote(
            ext.at[pl.ds(first, rows), rim_x], ext.at[pl.ds(first, rows), 17 * col],
            rim_send.at[i], rim_recv.at[i], side,
        )
        for i, first, rows in ((2, 1 + 3 * row, 5), (3, 6 - 5 * row, 3))
    ]
    rims[0].start()
    rims[1].start()

    rims[2].start()
    rims[3].start()
    loads[8].wait()
    loads[9].wait()

    def corner(band):
        return 4 * ((row + band) & 1), 8 * ((col + (band >> 1)) & 1)

    @jax.named_scope("conv")
    def conv(band):
        y0, c0 = corner(band)
        total = None
        for dy in range(3):
            for dx in range(3):
                cells = ext[pl.ds(y0 + dy, 4), pl.ds(c0 + dx, 8)].reshape(512, 256)
                term = dot(cells, cs[dy, dx])
                total = term if total is None else total + term
        act = (0.5 * total * (1.0 + jnp.tanh(0.5 * total))).astype(BF16)
        sp[band] = act
        for half in range(2):
            last = dot(pick[...], act[256 * half : 256 * half + 256])
            hsend[band, half] = last.astype(BF16)

    def tm_copy(band):
        return remote(
            hsend.at[band], hrecv.at[band], th_send.at[band], th_recv.at[band], tm_next
        )

    def shares(buffer, band, tokens):
        tokens = tokens.reshape(4, 8, 16, 256)
        for q in range(RING):
            buffer[band, q] = tokens[:, 2 * q : 2 * q + 2].reshape(128, 256)

    @jax.named_scope("temporal")
    def temporal(band):
        act = sp[band]
        wide = act.astype(F32).reshape(32, 16, 256)
        early = [dot(place[...], hrecv[band, half]) for half in range(2)]
        frame = iota((32, 16, 256), 1)
        total = dot(act, ct[0])
        for lag in (1, 2):
            before = [e[256 * (lag - 1) : 256 * lag] for e in early]
            before = jnp.concatenate(before, axis=0).reshape(32, 16, 256)
            moved = jnp.where(frame < lag, before, pltpu.roll(wide, lag, 1))
            total = total + dot(moved.astype(BF16).reshape(512, 256), ct[lag])
        y0, c0 = corner(band)
        own = xp[pl.ds(y0, 4), pl.ds(c0, 8)].reshape(512, 256).astype(F32)
        hid = (own + total).astype(BF16)
        shares(hidden, band, hid)
        v = hid.astype(F32)
        scale = lax.rsqrt(jnp.mean(v * v, axis=-1, keepdims=True) + 1e-6)
        shares(abuf, band, (v * scale * ag_ref[...]).astype(BF16))

    def a1_copy(band, k):
        to = lax.rem(ring + k, RING)
        return remote(
            abuf.at[band, to], xall.at[band, 2 + ring],
            a1_send.at[band, k - 1], a1_recv.at[band, k - 1], ring_at(k),
        )

    def forward(band, part):
        return remote(
            xall.at[band, 4 + part], xall.at[band, part],
            fw_send.at[band, part], fw_recv.at[band, part], group_next,
        )

    def send_out(band):
        for k in (2, 1, 3):
            a1_copy(band, k).start()

    @pl.loop(0, BANDS + LAG)
    def _(i):
        @pl.when(i < BANDS)
        def _():
            for step, rim in ((1, 0), (2, 2), (3, 1), (3, 3)):
                pl.when(i == step)(lambda rim=rim: rims[rim].wait())

            conv(i)
            pl.when(has_next)(lambda: tm_copy(i).start())

        @pl.when(i >= LAG)
        def _():
            band = i - LAG
            with jax.named_scope("tm_wait"):
                pl.when(has_prev)(lambda: tm_copy(band).wait_recv())
            temporal(band)
            pl.when(band < 2)(lambda: send_out(band))
            xall[band, 2 + ring] = abuf[band, ring]
            for part in (0, 1):
                pl.when(has_group_next & (ring == part + 2))(
                    lambda part=part: forward(band, part).start()
                )

    def a2_copy(band, k):
        to = lax.rem(ring + k, RING)
        return remote(
            mb.at[band, to], mback.at[band, ring],
            a2_send.at[band, k - 1], a2_recv.at[band, k - 1], ring_at(k),
        )

    for i in (10, 11, 12, 13):
        loads[i].wait()

    @jax.named_scope("keys_values")
    def keys_values(band, start, count):
        tokens = xall[band, start : start + count].reshape(count * 128, 256)
        for buffer, weight in ((kb, wqkv[1]), (vb, wqkv[2])):
            made = dot(tokens, weight).astype(BF16)
            buffer[band, start : start + count] = made.reshape(count, 8, 16, 256)

    @jax.named_scope("attend")
    def attend(band, half):
        jobs = [(cell, half) for cell in range(8)]
        zero = jnp.zeros((64, 128), BF16)

        def doubled(buffer, cell, half):
            rows = buffer[band, 2 * half : 2 * half + 4, cell].reshape(64, 256)
            upper = jnp.concatenate([rows[:, :128], zero], axis=1)
            return jnp.concatenate([upper, jnp.concatenate([zero, rows[:, 128:]], axis=1)], axis=0)

        expos = []
        for cell, half in jobs:
            query = qb[band, 2 * half : 2 * half + 2, cell]
            spread = (query[:, None] * hmask[...][None]).reshape(128, 256)
            scores = lax.dot_general(
                doubled(kb, cell, half), spread, (((1,), (1,)), ((), ())),
                preferred_element_type=F32,
            )
            scores = scores * (1.4426950408889634 * 32**-0.5) + bias[half]
            expos.append(scores.reshape(2, 64, 128))
        expos = [jnp.exp2(e - jnp.max(e, axis=1, keepdims=True)) for e in expos]
        norms = [1.0 / jnp.sum(e, axis=1, keepdims=True) for e in expos]
        head = (iota((2, 16, 256), 2) >> 5) & 3
        for (cell, half), expo, norm in zip(jobs, expos, norms):
            weights = (expo * norm).astype(BF16).reshape(128, 128)
            mixed = lax.dot_general(
                weights, doubled(vb, cell, half), (((0,), (0,)), ((), ())),
                preferred_element_type=F32,
            ).reshape(2, 4, 16, 256)
            own = mixed[:, 0]
            for h in range(1, 4):
                own = jnp.where(head == h, mixed[:, h], own)
            mb[band, 2 * half : 2 * half + 2, 16 * cell : 16 * cell + 16] = own.astype(BF16)

    def send_back(band, half):
        for k in (1, 2, 3):
            to = lax.rem(ring + k, RING)
            pl.when(lax.div(to, 2) == half)(lambda k=k: a2_copy(band, k).start())

        @pl.when(lax.div(ring, 2) == half)
        def _():
            mback[band, ring] = mb[band, ring]

    @jax.named_scope("a1_wait")
    def arrive(band, source):
        k = lax.rem(ring + RING - source, RING)

        @pl.when(k > 0)
        def _():
            a1_copy(band, k).wait_recv()
            if source >= 2:
                pl.when(has_group_next)(lambda: forward(band, source - 2).start())

    arrive(0, 3)
    arrive(0, 2)
    send_out(2)

    @pl.loop(0, BANDS + 1)
    def _(i):
        @pl.when(i < BANDS)
        def _():
            arrive(i, 1)
            arrive(i, 0)
            with jax.named_scope("queries"):
                tokens = xall[i, 2:6].reshape(512, 256)
                qb[i] = dot(tokens, wqkv[0]).astype(BF16).reshape(4, 8, 16, 256)
            keys_values(i, 2, 4)

        @pl.when(i < BANDS - 1)
        def _():
            arrive(i + 1, 3)
            arrive(i + 1, 2)
            pl.when(i == 0)(lambda: send_out(3))

        @pl.when(i >= 1)
        def _():
            band = i - 1
            with jax.named_scope("fw_wait"):
                for part in (0, 1):
                    pl.when(has_group_prev)(lambda part=part: forward(band, part).wait_recv())
            keys_values(band, 0, 2)
            attend(band, 0)
            send_back(band, 0)

        @pl.when(i < BANDS)
        def _():
            attend(i, 1)
            send_back(i, 1)

    def store(band):
        rows, columns = (pl.ds(start, size) for start, size in zip(corner(band), (4, 8)))
        return pltpu.make_async_copy(
            res.at[rows, columns], out_hbm.at[rows, columns], store_sem.at[band]
        )

    @pl.loop(0, BANDS)
    def _(band):
        with jax.named_scope('a2_wait'):
          for k in (1, 2, 3):
            a2_copy(band, k).wait()
        y0, c0 = corner(band)
        with jax.named_scope("outproj"):
            total = dot(mback[band].reshape(512, 256), wo[...])
            total = total + hidden[band].reshape(512, 256).astype(F32)
            total = total.astype(BF16).reshape(RING, 4, 2, 16, 256)
            for q in range(RING):
                res[pl.ds(y0, 4), pl.ds(c0 + 2 * q, 2)] = total[q]
        store(band).start()

    @pl.loop(0, BANDS)
    def _(band):
        pl.when(has_next)(lambda: tm_copy(band).wait_send())
        for part in (0, 1):
            pl.when(has_group_next)(lambda part=part: forward(band, part).wait_send())
        for k in (1, 2, 3):
            a1_copy(band, k).wait_send()

        store(band).wait()


def reorder(y_hbm, out_hbm, perm, res, ov, load_sem, store_sem):
    parts = [pl.ds(2 * i, 2) for i in range(4)]
    loads = [
        pltpu.make_async_copy(y_hbm.at[rows], res.at[rows], load_sem.at[i])
        for i, rows in enumerate(parts)
    ]
    stores = [
        pltpu.make_async_copy(ov.at[:, rows], out_hbm.at[:, rows], store_sem.at[i])
        for i, rows in enumerate(parts)
    ]
    for load in loads:
        load.start()
    perm[...] = swap()
    for i in range(4):
        loads[i].wait()
        for y in (2 * i, 2 * i + 1):
            o = dot(perm[...], res[y].reshape(256, 256)).astype(BF16)
            ov[:, y] = o.reshape(16, 16, 256)
        stores[i].start()
    for store in stores:
        store.wait()


def solution(mesh):
    tm_count = mesh.shape["tm"]

    def step(x, norm_gain, conv_space, conv_time, attn_gain, wq, wk, wv, wo):
        def vmem(*shape, dtype=BF16):
            return pltpu.VMEM(shape, dtype)

        dma = pltpu.SemaphoreType.DMA
        anywhere = pl.BlockSpec(memory_space=pltpu.HBM)
        here = pl.BlockSpec(memory_space=pltpu.VMEM)
        made = pl.pallas_call(
            functools.partial(kernel, tm_count),
            out_shape=jax.ShapeDtypeStruct((8, 16, 16, 256), BF16),
            in_specs=[
                anywhere, here, anywhere, anywhere, here,
                anywhere, anywhere, anywhere, anywhere,
            ],
            out_specs=anywhere,
            scratch_shapes=[
                vmem(16, 8, 16, 256), vmem(3, 3, 256, 256), vmem(3, 256, 256),
                vmem(3, 256, 256), vmem(256, 256),
                vmem(256, 256), vmem(32, 256), vmem(512, 32), vmem(2, 128, 128, dtype=F32),
                vmem(4, 16, 256),
                vmem(10, 18, 16, 256), vmem(8, 16, 16, 256), vmem(BANDS, 512, 256),
                vmem(BANDS, 2, 32, 256), vmem(BANDS, 2, 32, 256), vmem(BANDS, 4, 128, 256),
                vmem(BANDS, 4, 128, 256), vmem(BANDS, 6, 128, 256),
                vmem(BANDS, 4, 8, 16, 256), vmem(BANDS, 6, 8, 16, 256),
                vmem(BANDS, 6, 8, 16, 256), vmem(BANDS, 4, 128, 256),
                vmem(BANDS, 4, 128, 256), vmem(8, 16, 16, 256),
                dma((14,)), dma((BANDS,)), dma((4,)), dma((4,)), dma((BANDS,)), dma((BANDS,)),
                dma((BANDS, 3)), dma((BANDS, 3)), dma((BANDS, 2)), dma((BANDS, 2)),
                dma((BANDS, 3)), dma((BANDS, 3)),
            ],
            compiler_params=pltpu.CompilerParams(
                collective_id=0, has_side_effects=True, vmem_limit_bytes=60 << 20
            ),
            name="encoder_block",
        )(
            x, norm_gain.reshape(1, -1), conv_space, conv_time, attn_gain.reshape(1, -1),
            wq, wk, wv, wo,
        )
        return pl.pallas_call(
            reorder,
            out_shape=jax.ShapeDtypeStruct(x.shape, x.dtype),
            in_specs=[anywhere],
            out_specs=anywhere,
            scratch_shapes=[
                vmem(256, 256), vmem(8, 16, 16, 256), vmem(16, 8, 16, 256), dma((4,)), dma((4,)),
            ],
            compiler_params=pltpu.CompilerParams(vmem_limit_bytes=60 << 20),
            name="reorder",
        )(made)

    tile = P("tm", "row", "col", None)
    return jax.shard_map(
        step,
        mesh=mesh,
        in_specs=(tile, P(), P(), P(), P(), P(), P(), P(), P()),
        out_specs=tile,
        check_vma=False,
    )
```
